256 devices in a mesh: ctx: 32 (over y, x, core), head: 8 (over z).
Axes of the slice: x: 4, y: 4, z: 8, core: 2. Of those that a mesh axis runs over, the one named last changes fastest.
Arguments:
- query_rows: bfloat16 [16384, 8192], P('ctx', 'head'), may hold values from -6 to 6
- key_rows: bfloat16 [16384, 8192], P('ctx', 'head'), may hold values from -6 to 6
- value_rows: bfloat16 [16384, 8192], P('ctx', 'head'), may hold values from -18 to 18
- out_grad: bfloat16 [16384, 8192], P('ctx', 'head'), may hold values from -6 to 6
- norm_gain: float32 [8192], P('head'), may hold values from 0.5 to 2
- doc_ids: int32 [16384], P('ctx'), may hold values from 0 to 31, never falling along the last dimension, each value on 1 to 8192 neighbouring positions
Outputs:
- normed_out: bfloat16 [16384, 8192], P('ctx', 'head')
- query_grad: bfloat16 [16384, 8192], P('ctx', 'head')
- key_grad: bfloat16 [16384, 8192], P('ctx', 'head')
- value_grad: bfloat16 [16384, 8192], P('ctx', 'head')
The draws below stay inside these ranges and needn't reach their ends.
All inputs are finite; a program needn't handle non-finite values.
Results may differ from the reference program's by a relative error of at most 0.006.
Values sent between devices are 32-bit elements; how exact they have to be, the bound alone decides.
A program may use at most 128 MiB of HBM per device.

```python
import math
import jax
import jax.numpy as jnp
import numpy as np
from jax import lax

DH = 128
HEADS = 64
TOK_DEV = 512
TOKENS = 16384
DOCS = 32
N_CTX = 32


def draw_value_rows(key, part):
    key = jax.random.fold_in(key, 7)
    head_index = jnp.arange(HEADS * DH) // DH
    head_ramp = head_index.astype(jnp.float32) / max(HEADS - 1, 1)
    base_draw = jax.random.truncated_normal(key, -6.0, 6.0, (TOKENS, HEADS * DH), jnp.float32)
    head_scale = jnp.power(3.0, head_ramp)
    return (base_draw * head_scale[None, :]).astype(jnp.bfloat16)


def block_levels(stream_key, extent, pieces, smallest, top_value):
    loudness = 1.0
    for axis_at, blocks in pieces:
        draws = jax.random.uniform(jax.random.fold_in(jax.random.fold_in(stream_key, 6), axis_at), (blocks,), jnp.float32, smallest / len(pieces), top_value / len(pieces))
        loudness = loudness * jnp.repeat(jnp.exp(draws), extent[axis_at] // blocks).reshape((-1,) + (1,) * (len(extent) - 1 - axis_at))
    return loudness


def split_up(count, total, bound, lean):
    loads = [(1 << 20) // math.isqrt(grade ** lean) + 1 for grade in range(2, count + 1)]
    rest, given = total - bound - (count - 1), [1] * (count - 1)
    while rest > 0:
        movable = [i for i in range(count - 1) if given[i] < bound]
        whole, left = sum([loads[i] for i in movable]), rest
        for i in movable:
            addition = min(bound - given[i], max(1, left * loads[i] // whole), rest)
            given[i] = given[i] + addition
            rest = rest - addition
    return np.array([bound] + given)


def ragged(stream_key, count, total, bound, slope):
    if count == 2:
        one = jax.random.randint(stream_key, (), max(1, total - bound), min(bound, total - 1) + 1)
        return jnp.stack([one, total - one])
    sizes = jnp.asarray(split_up(count, total, bound, slope), jnp.int32)
    pairs = (count - 1) // 2
    giver, taker = sizes[1:1 + 2 * pairs:2], sizes[2:2 + 2 * pairs:2]
    room = jnp.minimum(giver - 1, bound - taker)
    moved = jax.random.randint(jax.random.fold_in(stream_key, 1), (pairs,), 0, 1 << 20) % (room + 1)
    sizes = sizes.at[1:1 + 2 * pairs:2].set(giver - moved).at[2:2 + 2 * pairs:2].set(taker + moved)
    return sizes[jax.random.permutation(jax.random.fold_in(stream_key, 2), count)]


def gaussian(own_key, shape, width, most, cuts=(), held_as=jnp.bfloat16):
    entries = jax.random.normal(own_key, shape, jnp.float32) * width
    if len(cuts) > 0:
        entries = block_levels(own_key, shape, cuts, -0.22, 0.18) * entries
    return jnp.clip(entries, min=-most, max=most).astype(held_as)


def setup_inputs(seed: int = 0) -> dict:
    arg_keys = jax.random.split(jax.random.key(seed), 7)
    query_rows = gaussian(arg_keys[0], (TOKENS, HEADS * DH), 1.0, 6.0, ((0, 32), (1, 8)))
    key_rows = gaussian(arg_keys[1], (TOKENS, HEADS * DH), 1.0, 6.0, ((0, 32), (1, 8)))
    value_rows = draw_value_rows(jax.random.fold_in(arg_keys[6], 71), 0)
    out_grad = gaussian(arg_keys[3], (TOKENS, HEADS * DH), 1.0, 6.0, ((0, 32), (1, 8)))
    norm_gain = jnp.clip(jnp.exp(math.log(2.0) - 1.3862944 * jax.random.uniform(arg_keys[4], (HEADS * DH,), jnp.float32) ** block_levels(arg_keys[4], (HEADS * DH,), ((0, 8),), -0.2, 0.2)), 0.5, 2.0)
    doc_ids = jnp.searchsorted(jnp.cumsum(ragged(arg_keys[5], DOCS, TOKENS, TOKENS // 2, 2)), jnp.arange(TOKENS), side="right").astype(jnp.int32)
    return {"query_rows": query_rows, "key_rows": key_rows, "value_rows": value_rows, "out_grad": out_grad, "norm_gain": norm_gain, "doc_ids": doc_ids}


epsilon = 1e-05

def as_float(array):
    return array.astype(jnp.float32)

def doc_mask(doc_block):
    positions = jnp.arange(doc_block.shape[0])
    return (doc_block[:, None] == doc_block[None, :]) & (positions[:, None] >= positions[None, :])

def block_scores(left, right, same_doc):
    raw_scores = jnp.einsum('thd,shd->hts', as_float(left), as_float(right))
    return jnp.where(same_doc[None], raw_scores, 0.0).astype(jnp.bfloat16)

def reference(query_rows, key_rows, value_rows, out_grad, norm_gain, doc_ids):
    block_shape = (N_CTX, TOK_DEV, HEADS, DH)
    queries = query_rows.reshape(block_shape)
    keyset = key_rows.reshape(block_shape)
    values = value_rows.reshape(block_shape)
    grads = out_grad.reshape(block_shape)
    doc_blocks = doc_ids.reshape(N_CTX, TOK_DEV)
    gain_heads = norm_gain.reshape(HEADS, DH)

    def forward_block(carry, inputs):
        state_carry, last_carry = carry
        query_b, key_b, value_b, grad_b, docs_b = inputs
        first_id = docs_b[0]
        last_id = docs_b[-1]
        incoming = jnp.where(last_carry == first_id, state_carry, 0.0)
        state_in = incoming.astype(jnp.bfloat16)
        same_doc = doc_mask(docs_b)
        weights = block_scores(query_b, key_b, same_doc)
        first_mask = (docs_b == first_id).astype(jnp.float32)[:, None, None]
        attended = jnp.einsum('hts,shd->thd', as_float(weights), as_float(value_b))
        attended = attended + jnp.einsum('thd,hde->the', as_float(query_b), as_float(state_in)) * first_mask
        last_mask = (docs_b == last_id).astype(jnp.bfloat16)[:, None, None]
        piece = jnp.einsum('shd,she->hde', as_float(key_b * last_mask), as_float(value_b))
        state_next = piece + jnp.where(first_id == last_id, incoming, 0.0)
        mean_sq = lax.optimization_barrier(jnp.mean(attended * attended, axis=(1, 2)))
        inv_rms = lax.rsqrt(mean_sq + epsilon)[:, None, None]
        normed = (gain_heads * attended * inv_rms).astype(jnp.bfloat16)
        scaled = gain_heads * as_float(grad_b)
        stat = lax.optimization_barrier(jnp.mean(scaled * attended, axis=(1, 2)))[:, None, None]
        out_adj = (inv_rms * scaled - attended * inv_rms * inv_rms * inv_rms * stat).astype(jnp.bfloat16)
        adj_weights = block_scores(out_adj, value_b, same_doc)
        query_grad = jnp.einsum('hts,shd->thd', as_float(adj_weights), as_float(key_b))
        query_grad = query_grad + jnp.einsum('the,hde->thd', as_float(out_adj), as_float(state_in)) * first_mask
        return ((state_next, last_id), (normed, query_grad.astype(jnp.bfloat16), out_adj))
    start = (jnp.zeros((HEADS, DH, DH), jnp.float32), jnp.int32(-1))
    _, (normed, query_grad, out_adj) = lax.scan(forward_block, start, (queries, keyset, values, grads, doc_blocks))

    def backward_block(carry, inputs):
        state_carry, first_carry = carry
        query_b, key_b, value_b, adj_b, docs_b = inputs
        first_id = docs_b[0]
        last_id = docs_b[-1]
        incoming = jnp.where(first_carry == last_id, state_carry, 0.0)
        state_back = incoming.astype(jnp.bfloat16)
        same_doc = doc_mask(docs_b)
        weights = block_scores(query_b, key_b, same_doc)
        adj_weights = block_scores(adj_b, value_b, same_doc)
        last_mask = (docs_b == last_id).astype(jnp.float32)[:, None, None]
        key_grad = jnp.einsum('hts,thd->shd', as_float(adj_weights), as_float(query_b))
        key_grad = key_grad + jnp.einsum('shd,hde->she', as_float(value_b), as_float(state_back)) * last_mask
        value_grad = jnp.einsum('hts,thd->shd', as_float(weights), as_float(adj_b))
        value_grad = value_grad + jnp.einsum('she,hde->shd', as_float(key_b), as_float(state_back)) * last_mask
        first_mask = (docs_b == first_id).astype(jnp.bfloat16)[:, None, None]
        piece = jnp.einsum('thd,the->hde', as_float(adj_b * first_mask), as_float(query_b))
        state_next = piece + jnp.where(first_id == last_id, incoming, 0.0)
        return ((state_next, first_id), (key_grad.astype(jnp.bfloat16), value_grad.astype(jnp.bfloat16)))
    _, (key_grad, value_grad) = lax.scan(backward_block, start, (queries, keyset, values, out_adj, doc_blocks), reverse=True)
    flat = (TOKENS, HEADS * DH)
    return (normed.reshape(flat), query_grad.reshape(flat), key_grad.reshape(flat), value_grad.reshape(flat))
```

```python
import functools

import jax
import jax.numpy as jnp
from jax import lax
from jax.experimental import pallas as pl
from jax.experimental.pallas import tpu as pltpu
from jax.sharding import PartitionSpec as P

DH = 128
TILE = 256
epsilon = 1e-05
MESH = pl.DeviceIdType.MESH
F32 = jnp.float32
BF16 = jnp.bfloat16


def nn(a, b):
    return lax.dot_general(a, b, (((1,), (0,)), ((), ())), preferred_element_type=F32)


def nt(a, b):
    return lax.dot_general(a, b, (((1,), (1,)), ((), ())), preferred_element_type=F32)


def tn(a, b):
    return lax.dot_general(a, b, (((0,), (0,)), ((), ())), preferred_element_type=F32)


def equal(a, b):
    return jnp.where(a == b, 1.0, 0.0).astype(F32)


def kernel(
    nctx, nhead,
    q_hbm, k_hbm, v_hbm, dy_hbm, gain_ref, docs_ref,
    normed_hbm, qg_hbm, kg_hbm, vg_hbm,
    q, k, v, dy, qf, kl, vl, oa, att, weights, adj, same, dcol,
    first_col, last_col, inv_col, adj_col, sq_acc, gr_acc,
    piece, sib_piece, total, slices, scanned, landed, to_sib, from_sib, state,
    my_info, sib_info, chip_info, all_info, stat_out, stat_in,
    normed, qg, kgl, vgl, kg, vg,
    in_sem, out_sem, info_send, info_recv, sib_info_sem,
    up_send, up_recv, a_send, a_recv, b_send, b_recv, down_send, down_recv,
    stat_send, stat_recv,
):
    tokens, width = q.shape
    heads = width // DH
    half = heads // 2
    chips = nctx // 2
    rows = half * DH // chips
    per_head = DH // rows
    blocks = tokens // DH
    tiles = tokens // TILE
    me = lax.axis_index("ctx")
    z = lax.axis_index("head")
    chip = lax.div(me, 2)
    core = lax.rem(me, 2)
    sibling = me + 1 - 2 * core
    shift = lax.rem(lax.div(chip, max(per_head, 1)), half)

    def cols(h):
        return pl.ds(pl.multiple_of(h * DH, DH), DH)

    def side(s):
        return pl.ds(pl.multiple_of(s * (width // 2), width // 2), width // 2)

    def slot(i):
        return pl.ds(pl.multiple_of(i * rows, rows), rows)

    def square(h):
        return pl.ds(pl.multiple_of(h * DH, DH), DH)

    def load(i, src, dst, s):
        return pltpu.make_async_copy(src.at[:, side(s)], dst.at[:, side(s)], in_sem.at[i])

    loads = [
        load(0, k_hbm, k, 1 - core), load(1, v_hbm, v, 1 - core),
        load(2, k_hbm, k, core), load(3, v_hbm, v, core),
        load(4, q_hbm, q, 0), load(5, q_hbm, q, 1),
        load(6, dy_hbm, dy, 0), load(7, dy_hbm, dy, 1),
    ]
    for copy in loads:
        copy.start()

    barrier = pltpu.get_barrier_semaphore()
    pl.semaphore_signal(barrier, inc=1, device_id={"ctx": sibling}, device_id_type=MESH)

    def greet_chip(d, carry):
        peer = lax.rem(chip + d, chips)
        pl.semaphore_signal(
            barrier, inc=1, device_id={"ctx": 2 * peer + core}, device_id_type=MESH
        )
        return carry

    def greet_head(d, carry):
        pl.semaphore_signal(
            barrier, inc=1, device_id={"head": lax.rem(z + d, nhead)}, device_id_type=MESH
        )
        return carry

    lax.fori_loop(1, chips, greet_chip, 0)
    lax.fori_loop(1, nhead, greet_head, 0)

    drow = docs_ref[...].astype(F32)
    first_id = drow[:, 0:1]
    last_id = drow[:, tokens - 1 : tokens]
    my_info[0:1, :] = jnp.broadcast_to(first_id, (1, DH))
    my_info[1:2, :] = jnp.broadcast_to(last_id, (1, DH))
    for b in range(blocks):
        block = slice(b * DH, (b + 1) * DH)
        dcol[block, :] = jnp.broadcast_to(drow[:, block], (DH, DH)).T
    first_col[...] = equal(dcol[...], first_id)
    last_col[...] = equal(dcol[...], last_id)

    def make_piece(h):
        last = last_col[...].astype(BF16)
        keys = k[:, cols(h)] * last
        kl[:, cols(h)] = keys
        vl[:, cols(h)] = v[:, cols(h)] * last
        piece[square(h), :] = tn(keys, v[:, cols(h)])

    def push_up(turn, j):
        return pltpu.make_async_remote_copy(
            src_ref=piece.at[square((1 - core) * half + j), :],
            dst_ref=sib_piece.at[turn, square(j), :],
            send_sem=up_send.at[turn, j],
            recv_sem=up_recv.at[turn, j],
            device_id={"ctx": sibling},
            device_id_type=MESH,
        )

    def send_slice(turn, i):
        return pltpu.make_async_remote_copy(
            src_ref=total.at[turn, slot(i), :],
            dst_ref=slices.at[turn, slot(chip), :],
            send_sem=a_send.at[turn, i],
            recv_sem=a_recv.at[turn, chip],
            device_id={"ctx": 2 * i + core},
            device_id_type=MESH,
        )

    def recv_slice(turn, i):
        return pltpu.make_async_remote_copy(
            src_ref=total.at[turn, slot(i), :],
            dst_ref=slices.at[turn, slot(i), :],
            send_sem=a_send.at[turn, i],
            recv_sem=a_recv.at[turn, i],
            device_id={"ctx": 2 * i + core},
            device_id_type=MESH,
        )

    def send_back(turn, i):
        return pltpu.make_async_remote_copy(
            src_ref=scanned.at[turn, slot(i), :],
            dst_ref=landed.at[turn, slot(chip), :],
            send_sem=b_send.at[turn, i],
            recv_sem=b_recv.at[turn, chip],
            device_id={"ctx": 2 * i + core},
            device_id_type=MESH,
        )

    def recv_back(turn, i):
        return pltpu.make_async_remote_copy(
            src_ref=scanned.at[turn, slot(i), :],
            dst_ref=landed.at[turn, slot(i), :],
            send_sem=b_send.at[turn, i],
            recv_sem=b_recv.at[turn, i],
            device_id={"ctx": 2 * i + core},
            device_id_type=MESH,
        )

    def push_down(turn, j):
        return pltpu.make_async_remote_copy(
            src_ref=to_sib.at[turn, square(j), :],
            dst_ref=from_sib.at[turn, square(j), :],
            send_sem=down_send.at[turn, j],
            recv_sem=down_recv.at[turn, j],
            device_id={"ctx": sibling},
            device_id_type=MESH,
        )

    def send_info(d):
        peer = lax.rem(chip + d, chips)
        return pltpu.make_async_remote_copy(
            src_ref=chip_info,
            dst_ref=all_info.at[chip],
            send_sem=info_send.at[peer],
            recv_sem=info_recv.at[chip],
            device_id={"ctx": 2 * peer + core},
            device_id_type=MESH,
        )

    def recv_info(i):
        return pltpu.make_async_remote_copy(
            src_ref=chip_info,
            dst_ref=all_info.at[i],
            send_sem=info_send.at[i],
            recv_sem=info_recv.at[i],
            device_id={"ctx": 2 * i + core},
            device_id_type=MESH,
        )

    def head_order(j):
        return lax.rem(j + shift, half)

    def orders(turn):
        return (0, 1, 2, 3) if turn == 0 else (3, 2, 1, 0)

    def is_near(turn):
        return jnp.full((1, DH), core if turn == 0 else 1 - core, jnp.int32) == 0

    def ascend(turn):
        near_first, near_last, far_first, far_last = orders(turn)
        joined = equal(chip_info[near_last : near_last + 1, :], chip_info[far_last : far_last + 1, :])
        mine = jnp.where(is_near(turn), joined, 1.0)
        theirs = jnp.where(is_near(turn), 1.0, joined)

        def one(j, carry):
            head = head_order(j)
            push_up(turn, head).wait_recv()
            total[turn, square(head), :] = (
                piece[square(core * half + head), :] * mine
                + sib_piece[turn, square(head), :] * theirs
            )
            for s in range(per_head):
                i = head * per_head + s

                @pl.when(i != chip)
                def _():
                    send_slice(turn, i).start()

                @pl.when(i == chip)
                def _():
                    slices[turn, slot(chip), :] = total[turn, slot(chip), :]

            return carry

        lax.fori_loop(0, half, one, 0)

    def scan(turn):
        near_first, _, _, far_last = orders(turn)

        def one(j, carry):
            running, before = carry
            i = j if turn == 0 else chips - 1 - j

            @pl.when(i != chip)
            def _():
                recv_slice(turn, i).wait_recv()

            ids = all_info[i]
            enters = ids[near_first : near_first + 1, :]
            leaves = ids[far_last : far_last + 1, :]
            arriving = running * equal(before, enters)
            scanned[turn, slot(i), :] = arriving

            @pl.when(i != chip)
            def _():
                send_back(turn, i).start()

            @pl.when(i == chip)
            def _():
                landed[turn, slot(chip), :] = arriving

            running = slices[turn, slot(i), :] + running * equal(before, leaves)
            return running, leaves

        lax.fori_loop(
            0, chips, one, (jnp.zeros((rows, DH), F32), jnp.full((1, DH), -1.0, F32))
        )

    def descend(turn):
        near_first, near_last, far_first, far_last = orders(turn)
        next_to = equal(chip_info[near_last : near_last + 1, :], chip_info[far_first : far_first + 1, :])
        through = equal(chip_info[near_first : near_first + 1, :], chip_info[far_first : far_first + 1, :])
        near = is_near(turn)
        own_enter = jnp.where(near, 1.0, through)
        own_sib = jnp.where(near, 0.0, next_to)
        sib_enter = jnp.where(near, through, 1.0)
        sib_own = jnp.where(near, next_to, 0.0)

        def one(j, carry):
            for s in range(per_head):
                i = j * per_head + s

                @pl.when(i != chip)
                def _():
                    recv_back(turn, i).wait_recv()

            entering = landed[turn, square(j), :]
            own = piece[square(core * half + j), :]
            theirs = sib_piece[turn, square(j), :]
            to_sib[turn, square(j), :] = entering * sib_enter + own * sib_own
            push_down(turn, j).start()
            state[turn, square(core * half + j), :] = (
                entering * own_enter + theirs * own_sib
            ).astype(BF16)
            return carry

        lax.fori_loop(0, half, one, 0)

    def land(turn, j):
        push_down(turn, j).wait_recv()
        state[turn, square((1 - core) * half + j), :] = from_sib[turn, square(j), :].astype(BF16)

    def settle(turn):
        def one_head(j, carry):
            push_up(turn, j).wait_send()
            push_down(turn, j).wait_send()
            return carry

        def one_chip(i, carry):
            @pl.when(i != chip)
            def _():
                send_slice(turn, i).wait_send()
                send_back(turn, i).wait_send()

            return carry

        lax.fori_loop(0, half, one_head, 0)
        lax.fori_loop(0, chips, one_chip, 0)

    loads[0].wait()
    loads[1].wait()

    def first_pieces(j, carry):
        make_piece((1 - core) * half + head_order(j))
        return carry

    lax.fori_loop(0, half, first_pieces, 0)
    pl.semaphore_wait(barrier, 1 + (chips - 1) + (nhead - 1))
    sib_ids = pltpu.make_async_remote_copy(
        src_ref=my_info,
        dst_ref=sib_info,
        send_sem=sib_info_sem.at[0],
        recv_sem=sib_info_sem.at[1],
        device_id={"ctx": sibling},
        device_id_type=MESH,
    )
    sib_ids.start()

    def start_up(j, carry):
        push_up(0, head_order(j)).start()
        return carry

    lax.fori_loop(0, half, start_up, 0)
    loads[2].wait()
    loads[3].wait()

    def own_pieces(j, carry):
        make_piece(core * half + head_order(j))
        return carry

    lax.fori_loop(0, half, own_pieces, 0)
    sib_ids.wait()
    near = is_near(0)
    for at in range(2):
        mine, theirs = my_info[at : at + 1, :], sib_info[at : at + 1, :]
        chip_info[at : at + 1, :] = jnp.where(near, mine, theirs)
        chip_info[at + 2 : at + 3, :] = jnp.where(near, theirs, mine)
    all_info[chip] = chip_info[...]

    def start_info(d, carry):
        send_info(d).start()
        return carry

    lax.fori_loop(1, chips, start_info, 0)
    ascend(0)

    for b in range(blocks):
        block = slice(b * DH, (b + 1) * DH)
        later = lax.broadcasted_iota(jnp.int32, (tokens, DH), 0)
        earlier = lax.broadcasted_iota(jnp.int32, (tokens, DH), 1) + b * DH
        ids = jnp.broadcast_to(drow[:, block], (tokens, DH))
        same[:, block] = jnp.where(
            (dcol[...] == ids) & (later >= earlier), 1.0, 0.0
        ).astype(BF16)
    for copy in loads[4:]:
        copy.wait()

    def local_forward(h, carry):
        qf[:, cols(h)] = q[:, cols(h)] * first_col[...].astype(BF16)
        for r in range(tiles):
            here, upto = slice(r * TILE, (r + 1) * TILE), slice(0, (r + 1) * TILE)
            scores = nt(q[here, cols(h)], k[upto, cols(h)])
            masked = scores.astype(BF16) * same[here, upto]
            weights[h, here, upto] = masked
            att[here, cols(h)] = nn(masked, v[upto, cols(h)])
        return carry

    lax.fori_loop(0, half, local_forward, 0)

    def wait_info(d, carry):
        recv_info(lax.rem(chip + d, chips)).wait_recv()
        return carry

    lax.fori_loop(1, chips, wait_info, 0)
    scan(0)
    lax.fori_loop(half, heads, local_forward, 0)
    descend(0)

    sq_acc[...] = jnp.zeros_like(sq_acc)
    gr_acc[...] = jnp.zeros_like(gr_acc)

    def attend(h):
        whole = att[:, cols(h)] + nn(qf[:, cols(h)], state[0, square(h), :])
        att[:, cols(h)] = whole
        scaled = gain_ref[:, cols(h)] * dy[:, cols(h)].astype(F32)
        sq_acc[...] += whole * whole
        gr_acc[...] += scaled * whole

    def attend_own(j, carry):
        attend(core * half + j)
        return carry

    def attend_other(j, carry):
        land(0, j)
        attend((1 - core) * half + j)
        return carry

    lax.fori_loop(0, half, attend_own, 0)
    lax.fori_loop(0, half, attend_other, 0)
    for b in range(blocks):
        block = slice(b * DH, (b + 1) * DH)
        stat_out[b : b + 1, :] = jnp.sum(sq_acc[block, :].T, axis=0, keepdims=True)
        stat_out[blocks + b : blocks + b + 1, :] = jnp.sum(
            gr_acc[block, :].T, axis=0, keepdims=True
        )
    stat_in[z] = stat_out[...]

    def send_stat(d):
        peer = lax.rem(z + d, nhead)
        return pltpu.make_async_remote_copy(
            src_ref=stat_out,
            dst_ref=stat_in.at[z],
            send_sem=stat_send.at[peer],
            recv_sem=stat_recv.at[z],
            device_id={"head": peer},
            device_id_type=MESH,
        )

    def recv_stat(d):
        source = lax.rem(z + nhead - d, nhead)
        return pltpu.make_async_remote_copy(
            src_ref=stat_out,
            dst_ref=stat_in.at[source],
            send_sem=stat_send.at[source],
            recv_sem=stat_recv.at[source],
            device_id={"head": source},
            device_id_type=MESH,
        )

    def start_stat(d, carry):
        send_stat(d).start()
        return carry

    def wait_stat(d, carry):
        recv_stat(d).wait_recv()
        return carry

    lax.fori_loop(1, nhead, start_stat, 0)
    settle(0)
    lax.fori_loop(1, nhead, wait_stat, 0)
    sums = stat_in[0]
    for other in range(1, nhead):
        sums = sums + stat_in[other]
    means = sums / (width * nhead)
    inv = lax.rsqrt(means[0:blocks, :] + epsilon)
    factor = inv * inv * inv * means[blocks : 2 * blocks, :]
    for b in range(blocks):
        block = slice(b * DH, (b + 1) * DH)
        inv_col[block, :] = jnp.broadcast_to(inv[b : b + 1, :], (DH, DH)).T
        adj_col[block, :] = jnp.broadcast_to(factor[b : b + 1, :], (DH, DH)).T

    def adjoint(h):
        scaled = gain_ref[:, cols(h)] * dy[:, cols(h)].astype(F32)
        grads = (inv_col[...] * scaled - att[:, cols(h)] * adj_col[...]).astype(BF16)
        oa[:, cols(h)] = grads
        piece[square(h), :] = tn(grads, qf[:, cols(h)])

    def adjoint_other(j, carry):
        head = head_order(j)
        adjoint((1 - core) * half + head)
        push_up(1, head).start()
        return carry

    def adjoint_own(j, carry):
        adjoint(core * half + head_order(j))
        return carry

    lax.fori_loop(0, half, adjoint_other, 0)
    lax.fori_loop(0, half, adjoint_own, 0)
    ascend(1)

    def local_backward(h, carry):
        grads = oa[:, cols(h)]
        stepped = nt(grads, state[0, square(h), :]) * first_col[...]
        for r in range(tiles):
            here, upto = slice(r * TILE, (r + 1) * TILE), slice(0, (r + 1) * TILE)
            scores = nt(grads[here], v[upto, cols(h)])
            masked = scores.astype(BF16) * same[here, upto]
            adj[here, upto] = masked
            qg[here, cols(h)] = (nn(masked, k[upto, cols(h)]) + stepped[here]).astype(BF16)
        for r in range(tiles):
            here, onward = slice(r * TILE, (r + 1) * TILE), slice(r * TILE, tokens)
            kgl[here, cols(h)] = tn(adj[onward, here], q[onward, cols(h)])
            vgl[here, cols(h)] = tn(weights[h, onward, here], grads[onward])
        normed[:, cols(h)] = (gain_ref[:, cols(h)] * att[:, cols(h)] * inv_col[...]).astype(BF16)
        return carry

    lax.fori_loop(0, half, local_backward, 0)
    scan(1)
    lax.fori_loop(half, heads, local_backward, 0)
    stores = [
        pltpu.make_async_copy(normed, normed_hbm, out_sem.at[0]),
        pltpu.make_async_copy(qg, qg_hbm, out_sem.at[1]),
    ]
    for copy in stores:
        copy.start()
    descend(1)

    def finish(h):
        back = state[1, square(h), :]
        kg[:, cols(h)] = (kgl[:, cols(h)] + nn(vl[:, cols(h)], back)).astype(BF16)
        vg[:, cols(h)] = (vgl[:, cols(h)] + nt(kl[:, cols(h)], back)).astype(BF16)

    def finish_own(j, carry):
        finish(core * half + j)
        return carry

    def finish_other(j, carry):
        land(1, j)
        finish((1 - core) * half + j)
        return carry

    def store(i, src, dst, s):
        return pltpu.make_async_copy(src.at[:, side(s)], dst.at[:, side(s)], out_sem.at[i])

    lax.fori_loop(0, half, finish_own, 0)
    for i, (src, dst) in enumerate(((kg, kg_hbm), (vg, vg_hbm))):
        stores.append(store(2 + i, src, dst, core))
        stores[-1].start()
    lax.fori_loop(0, half, finish_other, 0)
    for i, (src, dst) in enumerate(((kg, kg_hbm), (vg, vg_hbm))):
        stores.append(store(4 + i, src, dst, 1 - core))
        stores[-1].start()

    settle(1)

    def end_info(d, carry):
        send_info(d).wait_send()
        return carry

    def end_stat(d, carry):
        send_stat(d).wait_send()
        return carry

    lax.fori_loop(1, chips, end_info, 0)
    lax.fori_loop(1, nhead, end_stat, 0)
    for copy in stores:
        copy.wait()


def body(nctx, nhead, query_rows, key_rows, value_rows, out_grad, norm_gain, doc_ids):
    tokens, width = query_rows.shape
    heads = width // DH
    half = heads // 2
    chips = nctx // 2
    blocks = tokens // DH
    grid = (tokens, width)
    dma = pltpu.SemaphoreType.DMA
    scratch = [
        *[pltpu.VMEM(grid, BF16)] * 4,
        *[pltpu.VMEM(grid, BF16)] * 4,
        pltpu.VMEM(grid, F32),
        pltpu.VMEM((heads, tokens, tokens), BF16),
        pltpu.VMEM((tokens, tokens), BF16),
        pltpu.VMEM((tokens, tokens), BF16),
        *[pltpu.VMEM((tokens, DH), F32)] * 7,
        pltpu.VMEM((heads * DH, DH), F32),
        *[pltpu.VMEM((2, half * DH, DH), F32)] * 7,
        pltpu.VMEM((2, heads * DH, DH), BF16),
        *[pltpu.VMEM((8, DH), F32)] * 3,
        pltpu.VMEM((chips, 8, DH), F32),
        pltpu.VMEM((2 * blocks, DH), F32),
        pltpu.VMEM((nhead, 2 * blocks, DH), F32),
        *[pltpu.VMEM(grid, BF16)] * 2,
        *[pltpu.VMEM(grid, F32)] * 2,
        *[pltpu.VMEM(grid, BF16)] * 2,
        dma((8,)), dma((6,)), dma((chips,)), dma((chips,)), dma((2,)),
        dma((2, half)), dma((2, half)), dma((2, chips)), dma((2, chips)),
        dma((2, chips)), dma((2, chips)), dma((2, half)), dma((2, half)),
        dma((nhead,)), dma((nhead,)),
    ]
    anywhere = pl.BlockSpec(memory_space=pl.ANY)
    in_vmem = pl.BlockSpec(memory_space=pltpu.VMEM)
    return pl.pallas_call(
        functools.partial(kernel, nctx, nhead),
        out_shape=[jax.ShapeDtypeStruct(grid, BF16)] * 4,
        in_specs=[anywhere] * 4 + [in_vmem] * 2,
        out_specs=[anywhere] * 4,
        scratch_shapes=scratch,
        compiler_params=pltpu.CompilerParams(
            collective_id=0, has_side_effects=True, vmem_limit_bytes=50 * 2**20
        ),
        name="attend",
    )(
        query_rows, key_rows, value_rows, out_grad,
        norm_gain.reshape(1, width), doc_ids.reshape(1, tokens),
    )


def solution(mesh):
    nctx, nhead = mesh.shape["ctx"], mesh.shape["head"]
    placed = (
        P("ctx", "head"),
        P("ctx", "head"),
        P("ctx", "head"),
        P("ctx", "head"),
        P("head"),
        P("ctx"),
    )
    return jax.shard_map(
        functools.partial(body, nctx, nhead),
        mesh=mesh,
        in_specs=placed,
        out_specs=(P("ctx", "head"), P("ctx", "head"), P("ctx", "head"), P("ctx", "head")),
        check_vma=False,
    )
```

```python
import functools
import math

import jax
import jax.numpy as jnp
from jax import lax
from jax.experimental import pallas as pl
from jax.experimental.pallas import tpu as pltpu
from jax.sharding import PartitionSpec as P

DH = 128
TILE = 256
epsilon = 1e-05
MESH = pl.DeviceIdType.MESH
F32 = jnp.float32
BF16 = jnp.bfloat16


def nn(a, b):
    return lax.dot_general(a, b, (((1,), (0,)), ((), ())), preferred_element_type=F32)


def nt(a, b):
    return lax.dot_general(a, b, (((1,), (1,)), ((), ())), preferred_element_type=F32)


def tn(a, b):
    return lax.dot_general(a, b, (((0,), (0,)), ((), ())), preferred_element_type=F32)


def equal(a, b):
    return jnp.where(a == b, 1.0, 0.0).astype(F32)


def far_first(chips):
    across = math.isqrt(chips)
    along = chips // across

    def hops(offset):
        dy, dx = offset
        return min(dy, along - dy) + min(dx, across - dx)

    offsets = [(dy, dx) for dy in range(along) for dx in range(across) if dy + dx > 0]
    return sorted(offsets, key=hops, reverse=True)


def kernel(
    nctx, nhead,
    q_hbm, k_hbm, v_hbm, dy_hbm, gain_hbm, docs_hbm,
    normed, qg, kgl0, kgl1, vgl0, vgl1, kl, vl, back_state,
    q, k, v, dy, qf, oa, att, weights, adj, same, gain, docs, qf_turned, dcol,
    first_col, last_col, inv_col, adj_col, sq_acc, gr_acc,
    piece, sib_piece, total, slices, scanned, landed, to_sib, from_sib, state,
    my_info, sib_info, chip_info, all_info, stat_out, stat_in,
    in_sem, info_sem, sib_sem, up_send, up_recv, a_send, a_recv, b_send, b_recv,
    down_send, down_recv, stat_sem,
):
    tokens, width = q.shape
    heads = width // DH
    half = heads // 2
    chips = nctx // 2
    across = math.isqrt(chips)
    along = chips // across
    rows = half * DH // chips
    blocks = tokens // DH
    tiles = tokens // TILE
    me = lax.axis_index("ctx")
    z = lax.axis_index("head")
    chip = lax.div(me, 2)
    core = lax.rem(me, 2)
    sibling = me + 1 - 2 * core
    mine, other = core * half, (1 - core) * half
    everyone = (chips - 1) * rows

    def cols(h):
        return pl.ds(pl.multiple_of(h * DH, DH), DH)

    def side(s):
        return pl.ds(pl.multiple_of(s * (width // 2), width // 2), width // 2)

    def slot(i):
        return pl.ds(pl.multiple_of(i * rows, rows), rows)

    def half_of(h):
        return pl.ds(pl.multiple_of(h * DH, half * DH), half * DH)

    def chip_at(offset):
        y = lax.rem(lax.div(chip, across) + offset[0], along)
        x = lax.rem(lax.rem(chip, across) + offset[1], across)
        return y * across + x

    def to_chip(i):
        return {"ctx": 2 * i + core}

    chip_offsets = far_first(chips)
    head_offsets = sorted(range(1, nhead), key=lambda d: -min(d, nhead - d))

    def load(i, src, dst, s):
        return pltpu.make_async_copy(src.at[:, side(s)], dst.at[:, side(s)], in_sem.at[i])

    first_loads = [load(0, k_hbm, k, 1 - core), load(1, v_hbm, v, 1 - core)]
    docs_load = pltpu.make_async_copy(docs_hbm, docs, in_sem.at[2])
    own_loads = [load(3, k_hbm, k, core), load(4, v_hbm, v, core)]
    later_loads = [
        pltpu.make_async_copy(q_hbm, q, in_sem.at[5]),
        pltpu.make_async_copy(dy_hbm, dy, in_sem.at[6]),
        pltpu.make_async_copy(gain_hbm, gain, in_sem.at[7]),
    ]
    docs_load.start()
    for copy in first_loads:
        copy.start()

    barrier = pltpu.get_barrier_semaphore()

    def greet(device):
        pl.semaphore_signal(barrier, inc=1, device_id=device, device_id_type=MESH)

    for offset in chip_offsets:
        greet(to_chip(chip_at(offset)))
    for offset in head_offsets:
        greet({"head": lax.rem(z + offset, nhead)})
    greet({"ctx": sibling})
    for copy in own_loads + later_loads:
        copy.start()

    docs_load.wait()
    drow = docs[...].astype(F32)
    first_id = drow[:, 0:1]
    last_id = drow[:, tokens - 1 : tokens]
    my_info[0:1, :] = jnp.broadcast_to(first_id, (1, DH))
    my_info[1:2, :] = jnp.broadcast_to(last_id, (1, DH))
    for b in range(blocks):
        block = slice(b * DH, (b + 1) * DH)
        dcol[block, :] = jnp.broadcast_to(drow[:, block], (DH, DH)).T
    first_col[...] = equal(dcol[...], first_id)
    last_col[...] = equal(dcol[...], last_id).astype(BF16)

    def to_sibling(src, dst, send_sem, recv_sem):
        return pltpu.make_async_remote_copy(
            src_ref=src,
            dst_ref=dst,
            send_sem=send_sem,
            recv_sem=recv_sem,
            device_id={"ctx": sibling},
            device_id_type=MESH,
        )

    def push_up(turn):
        return to_sibling(
            piece.at[turn, half_of(other), :], sib_piece.at[turn],
            up_send.at[turn], up_recv.at[turn],
        )

    def push_down(turn):
        return to_sibling(
            to_sib.at[turn], from_sib.at[turn], down_send.at[turn], down_recv.at[turn]
        )

    def spread(src, dst, send_sem, recv_sem):
        for offset in chip_offsets:
            i = chip_at(offset)
            pltpu.make_async_remote_copy(
                src_ref=src.at[slot(i), :],
                dst_ref=dst.at[slot(chip), :],
                send_sem=send_sem,
                recv_sem=recv_sem,
                device_id=to_chip(i),
                device_id_type=MESH,
            ).start()

    def spread_whole(src, dst, send_sem, recv_sem):
        return pltpu.make_async_remote_copy(
            src_ref=src.at[0:everyone, :],
            dst_ref=dst.at[0:everyone, :],
            send_sem=send_sem,
            recv_sem=recv_sem,
            device_id={"ctx": sibling},
            device_id_type=MESH,
        )

    def slices_whole(turn):
        return spread_whole(total.at[turn], slices.at[turn], a_send.at[turn], a_recv.at[turn])

    def back_whole(turn):
        return spread_whole(scanned.at[turn], landed.at[turn], b_send.at[turn], b_recv.at[turn])

    def info_whole():
        return pltpu.make_async_remote_copy(
            src_ref=all_info.at[0 : chips - 1],
            dst_ref=all_info.at[0 : chips - 1],
            send_sem=info_sem.at[0],
            recv_sem=info_sem.at[1],
            device_id={"ctx": sibling},
            device_id_type=MESH,
        )

    def orders(turn):
        return (0, 1, 2, 3) if turn == 0 else (3, 2, 1, 0)

    def is_near(turn):
        return jnp.full((1, DH), core if turn == 0 else 1 - core, jnp.int32) == 0

    def ids_of(row):
        return chip_info[row : row + 1, :]

    def ascend(turn):
        _, near_last, _, far_last = orders(turn)
        joined = equal(ids_of(near_last), ids_of(far_last))
        own_share = jnp.where(is_near(turn), joined, 1.0)
        sib_share = jnp.where(is_near(turn), 1.0, joined)
        push_up(turn).wait_recv()
        total[turn] = piece[turn, half_of(mine), :] * own_share + sib_piece[turn] * sib_share
        spread(total.at[turn], slices.at[turn], a_send.at[turn], a_recv.at[turn])
        slices[turn, slot(chip), :] = total[turn, slot(chip), :]

    def scan(turn):
        near_first, _, _, far_last = orders(turn)
        slices_whole(turn).wait_recv()
        running = jnp.zeros((rows, DH), F32)
        before = jnp.full((1, DH), -1.0, F32)
        for j in range(chips):
            i = j if turn == 0 else chips - 1 - j
            ids = all_info[i]
            enters = ids[near_first : near_first + 1, :]
            leaves = ids[far_last : far_last + 1, :]
            here = slice(i * rows, (i + 1) * rows)
            scanned[turn, here, :] = running * equal(before, enters)
            running = slices[turn, here, :] + running * equal(before, leaves)
            before = leaves
        spread(scanned.at[turn], landed.at[turn], b_send.at[turn], b_recv.at[turn])
        landed[turn, slot(chip), :] = scanned[turn, slot(chip), :]

    def descend(turn, into):
        near_first, near_last, far_first, _ = orders(turn)
        next_to = equal(ids_of(near_last), ids_of(far_first))
        through = equal(ids_of(near_first), ids_of(far_first))
        near = is_near(turn)
        own_enter = jnp.where(near, 1.0, through)
        own_sib = jnp.where(near, 0.0, next_to)
        sib_enter = jnp.where(near, through, 1.0)
        sib_own = jnp.where(near, next_to, 0.0)
        back_whole(turn).wait_recv()
        to_sib[turn] = landed[turn] * sib_enter + piece[turn, half_of(mine), :] * sib_own
        push_down(turn).start()
        into[half_of(mine), :] = (landed[turn] * own_enter + sib_piece[turn] * own_sib).astype(BF16)

    def land(turn, into):
        push_down(turn).wait_recv()
        into[half_of(other), :] = from_sib[turn].astype(BF16)

    def settle(turn):
        push_up(turn).wait_send()
        push_down(turn).wait_send()
        slices_whole(turn).wait_send()
        back_whole(turn).wait_send()

    def make_piece(h):
        piece[0, cols(h), :] = tn(k[:, cols(h)] * last_col[...], v[:, cols(h)])

    for copy in first_loads:
        copy.wait()
    for j in range(half):
        make_piece(other + j)
    pl.semaphore_wait(barrier, 1 + (chips - 1) + (nhead - 1))
    sib_ids = to_sibling(my_info, sib_info, sib_sem.at[0], sib_sem.at[1])
    sib_ids.start()
    push_up(0).start()
    for copy in own_loads:
        copy.wait()
    for j in range(half):
        make_piece(mine + j)
    sib_ids.wait_recv()
    near = is_near(0)
    for at in range(2):
        here, there = my_info[at : at + 1, :], sib_info[at : at + 1, :]
        chip_info[at : at + 1, :] = jnp.where(near, here, there)
        chip_info[at + 2 : at + 3, :] = jnp.where(near, there, here)
    for offset in chip_offsets:
        pltpu.make_async_remote_copy(
            src_ref=chip_info,
            dst_ref=all_info.at[chip],
            send_sem=info_sem.at[0],
            recv_sem=info_sem.at[1],
            device_id=to_chip(chip_at(offset)),
            device_id_type=MESH,
        ).start()
    all_info[chip] = chip_info[...]
    ascend(0)

    later = lax.broadcasted_iota(jnp.int32, (tokens, DH), 0)
    for b in range(blocks):
        block = slice(b * DH, (b + 1) * DH)
        earlier = lax.broadcasted_iota(jnp.int32, (tokens, DH), 1) + b * DH
        ids = jnp.broadcast_to(drow[:, block], (tokens, DH))
        same[:, block] = jnp.where((dcol[...] == ids) & (later >= earlier), 1.0, 0.0).astype(BF16)
    for copy in later_loads:
        copy.wait()

    def local_forward(h, carry):
        kl[:, cols(h)] = k[:, cols(h)] * last_col[...]
        vl[:, cols(h)] = v[:, cols(h)] * last_col[...]
        firsts = q[:, cols(h)] * first_col[...].astype(BF16)
        qf[:, cols(h)] = firsts
        qf_turned[cols(h), :] = firsts.T
        for r in range(tiles):
            here, upto = slice(r * TILE, (r + 1) * TILE), slice(0, (r + 1) * TILE)
            scores = nt(q[here, cols(h)], k[upto, cols(h)])
            masked = scores.astype(BF16) * same[here, upto]
            weights[h, here, upto] = masked
            att[here, cols(h)] = nn(masked, v[upto, cols(h)])
        return carry

    lax.fori_loop(0, heads, local_forward, 0, unroll=2)
    info_whole().wait_recv()
    scan(0)
    descend(0, state)

    def attend(h, first):
        whole = att[:, cols(h)] + nn(qf[:, cols(h)], state[cols(h), :])
        att[:, cols(h)] = whole
        scaled = gain[:, cols(h)] * dy[:, cols(h)].astype(F32)
        squares, grads = whole * whole, scaled * whole
        sq_acc[...] = squares if first else sq_acc[...] + squares
        gr_acc[...] = grads if first else gr_acc[...] + grads

    for j in range(half):
        attend(mine + j, j == 0)
    land(0, state)
    for j in range(half):
        attend(other + j, False)
    for b in range(blocks):
        block = slice(b * DH, (b + 1) * DH)
        stat_out[b : b + 1, :] = jnp.sum(sq_acc[block, :].T, axis=0, keepdims=True)
        stat_out[blocks + b : blocks + b + 1, :] = jnp.sum(
            gr_acc[block, :].T, axis=0, keepdims=True
        )
    for offset in head_offsets:
        pltpu.make_async_remote_copy(
            src_ref=stat_out,
            dst_ref=stat_in.at[z],
            send_sem=stat_sem.at[0],
            recv_sem=stat_sem.at[1],
            device_id={"head": lax.rem(z + offset, nhead)},
            device_id_type=MESH,
        ).start()
    stat_in[z] = stat_out[...]
    settle(0)
    stat_whole = pltpu.make_async_remote_copy(
        src_ref=stat_in.at[0 : nhead - 1],
        dst_ref=stat_in.at[0 : nhead - 1],
        send_sem=stat_sem.at[0],
        recv_sem=stat_sem.at[1],
        device_id={"ctx": sibling},
        device_id_type=MESH,
    )
    stat_whole.wait_recv()
    sums = stat_in[0]
    for at in range(1, nhead):
        sums = sums + stat_in[at]
    means = sums / (width * nhead)
    inv = lax.rsqrt(means[0:blocks, :] + epsilon)
    factor = inv * inv * inv * means[blocks : 2 * blocks, :]
    for b in range(blocks):
        block = slice(b * DH, (b + 1) * DH)
        inv_col[block, :] = jnp.broadcast_to(inv[b : b + 1, :], (DH, DH)).T
        adj_col[block, :] = jnp.broadcast_to(factor[b : b + 1, :], (DH, DH)).T

    def adjoint(h):
        scaled = gain[:, cols(h)] * dy[:, cols(h)].astype(F32)
        grads = (inv_col[...] * scaled - att[:, cols(h)] * adj_col[...]).astype(BF16)
        oa[:, cols(h)] = grads
        piece[1, cols(h), :] = nn(qf_turned[cols(h), :], grads)

    for j in range(half):
        adjoint(other + j)
    push_up(1).start()
    for j in range(half):
        adjoint(mine + j)
    ascend(1)

    def local_backward(j, carry, base, kgl, vgl):
        h = base + j
        grads = oa[:, cols(h)]
        stepped = nt(grads, state[cols(h), :]) * first_col[...]
        for r in range(tiles):
            here, upto = slice(r * TILE, (r + 1) * TILE), slice(0, (r + 1) * TILE)
            scores = nt(grads[here], v[upto, cols(h)])
            masked = scores.astype(BF16) * same[here, upto]
            adj[here, upto] = masked
            qg[here, cols(h)] = (nn(masked, k[upto, cols(h)]) + stepped[here]).astype(BF16)
        for r in range(tiles):
            here, onward = slice(r * TILE, (r + 1) * TILE), slice(r * TILE, tokens)
            kgl[here, cols(j)] = tn(adj[onward, here], q[onward, cols(h)])
            vgl[here, cols(j)] = tn(weights[h, onward, here], grads[onward])
        normed[:, cols(h)] = (gain[:, cols(h)] * att[:, cols(h)] * inv_col[...]).astype(BF16)
        return carry

    lower = functools.partial(local_backward, base=0, kgl=kgl0, vgl=vgl0)
    upper = functools.partial(local_backward, base=half, kgl=kgl1, vgl=vgl1)
    lax.fori_loop(0, half, lower, 0, unroll=2)
    scan(1)
    lax.fori_loop(0, half, upper, 0, unroll=2)
    descend(1, back_state)
    sib_ids.wait_send()
    info_whole().wait_send()
    stat_whole.wait_send()
    land(1, back_state)
    settle(1)


def finish(
    normed, qg, kgl0, kgl1, vgl0, vgl1, kl, vl, back_state,
    normed_hbm, qg_hbm, kg_hbm, vg_hbm,
    kg, vg, out_sem,
):
    heads = kg.shape[1] // DH
    stores = [
        pltpu.make_async_copy(normed, normed_hbm, out_sem.at[0]),
        pltpu.make_async_copy(qg, qg_hbm, out_sem.at[1]),
    ]
    for copy in stores:
        copy.start()
    parts = 2
    per_part = heads // parts
    for part, (kgl, vgl) in enumerate(((kgl0, vgl0), (kgl1, vgl1))):
        for j in range(per_part):
            here = slice(j * DH, (j + 1) * DH)
            at = slice((part * per_part + j) * DH, (part * per_part + j + 1) * DH)
            back = back_state[at, :]
            kg[:, at] = (kgl[:, here] + nt(vl[:, at], back)).astype(BF16)
            vg[:, at] = (vgl[:, here] + nn(kl[:, at], back)).astype(BF16)
        done = slice(part * per_part * DH, (part + 1) * per_part * DH)
        for i, (src, dst) in enumerate(((kg, kg_hbm), (vg, vg_hbm))):
            copy = pltpu.make_async_copy(
                src.at[:, done], dst.at[:, done], out_sem.at[2 + 2 * part + i]
            )
            copy.start()
            stores.append(copy)
    for copy in stores:
        copy.wait()


def body(nctx, nhead, query_rows, key_rows, value_rows, out_grad, norm_gain, doc_ids):
    tokens, width = query_rows.shape
    heads = width // DH
    half = heads // 2
    chips = nctx // 2
    blocks = tokens // DH
    grid = (tokens, width)
    dma = pltpu.SemaphoreType.DMA
    scratch = [
        *[pltpu.VMEM(grid, BF16)] * 6,
        pltpu.VMEM(grid, F32),
        pltpu.VMEM((heads, tokens, tokens), BF16),
        pltpu.VMEM((tokens, tokens), BF16),
        pltpu.VMEM((tokens, tokens), BF16),
        pltpu.VMEM((1, width), F32),
        pltpu.VMEM((1, tokens), jnp.int32),
        pltpu.VMEM((heads * DH, tokens), BF16),
        *[pltpu.VMEM((tokens, DH), F32)] * 2,
        pltpu.VMEM((tokens, DH), BF16),
        *[pltpu.VMEM((tokens, DH), F32)] * 4,
        pltpu.VMEM((2, heads * DH, DH), F32),
        *[pltpu.VMEM((2, half * DH, DH), F32)] * 7,
        pltpu.VMEM((heads * DH, DH), BF16),
        *[pltpu.VMEM((8, DH), F32)] * 3,
        pltpu.VMEM((chips, 8, DH), F32),
        pltpu.VMEM((2 * blocks, DH), F32),
        pltpu.VMEM((nhead, 2 * blocks, DH), F32),
        dma((8,)),
        *[dma((2,))] * 11,
    ]
    arrays = (
        query_rows, key_rows, value_rows, out_grad,
        norm_gain.reshape(1, width), doc_ids.reshape(1, tokens),
    )
    anywhere = pl.BlockSpec(memory_space=pl.ANY)
    in_hbm = pl.BlockSpec(memory_space=pltpu.HBM)
    in_vmem = pl.BlockSpec(memory_space=pltpu.VMEM)
    parts = pl.pallas_call(
        functools.partial(kernel, nctx, nhead),
        out_shape=[
            *[jax.ShapeDtypeStruct(grid, BF16)] * 2,
            *[jax.ShapeDtypeStruct((tokens, width // 2), F32)] * 4,
            *[jax.ShapeDtypeStruct(grid, BF16)] * 2,
            jax.ShapeDtypeStruct((heads * DH, DH), BF16),
        ],
        in_specs=[in_hbm] * 6,
        out_specs=[in_vmem] * 9,
        scratch_shapes=scratch,
        compiler_params=pltpu.CompilerParams(
            collective_id=0, has_side_effects=True, vmem_limit_bytes=44 * 2**20
        ),
        name="attend",
    )(*[pltpu.with_memory_space_constraint(array, pltpu.HBM) for array in arrays])
    return pl.pallas_call(
        finish,
        out_shape=[jax.ShapeDtypeStruct(grid, BF16)] * 4,
        in_specs=[in_vmem] * 9,
        out_specs=[anywhere] * 4,
        scratch_shapes=[*[pltpu.VMEM(grid, BF16)] * 2, dma((6,))],
        compiler_params=pltpu.CompilerParams(vmem_limit_bytes=16 * 2**20),
        name="finish",
    )(*parts)


def solution(mesh):
    nctx, nhead = mesh.shape["ctx"], mesh.shape["head"]
    placed = (
        P("ctx", "head"),
        P("ctx", "head"),
        P("ctx", "head"),
        P("ctx", "head"),
        P("head"),
        P("ctx"),
    )
    return jax.shard_map(
        functools.partial(body, nctx, nhead),
        mesh=mesh,
        in_specs=placed,
        out_specs=(P("ctx", "head"), P("ctx", "head"), P("ctx", "head"), P("ctx", "head")),
        check_vma=False,
    )
```

```python
import functools
import math

import jax
import jax.numpy as jnp
from jax import lax
from jax.experimental import pallas as pl
from jax.experimental.pallas import tpu as pltpu
from jax.sharding import PartitionSpec as P

DH = 128
TILE = 256
epsilon = 1e-05
MESH = pl.DeviceIdType.MESH
F32 = jnp.float32
BF16 = jnp.bfloat16


def nn(a, b):
    return lax.dot_general(a, b, (((1,), (0,)), ((), ())), preferred_element_type=F32)


def nt(a, b):
    return lax.dot_general(a, b, (((1,), (1,)), ((), ())), preferred_element_type=F32)


def tn(a, b):
    return lax.dot_general(a, b, (((0,), (0,)), ((), ())), preferred_element_type=F32)


def equal(a, b):
    return jnp.where(a == b, 1.0, 0.0).astype(F32)


def row_sums(values):
    ones = jnp.ones((8, DH), BF16)
    high = values.astype(BF16)
    low = (values - high.astype(F32)).astype(BF16)
    return (nt(ones, high) + nt(ones, low))[0:1, :]


def far_first(chips):
    across = math.isqrt(chips)
    along = chips // across

    def hops(offset):
        dy, dx = offset
        return min(dy, along - dy) + min(dx, across - dx)

    offsets = [(dy, dx) for dy in range(along) for dx in range(across) if dy + dx > 0]
    return sorted(offsets, key=hops, reverse=True)


def kernel(
    nctx, nhead,
    q_hbm, k_hbm, v_hbm, dy_hbm, gain_hbm, docs_hbm,
    normed, qg, kg_own, vg_own, kgl_other, vgl_other, kl_other, vl_other, back_other,
    q, k, v, dy, qf, oa, att, scaled, weights, adj, same, gain, docs, qf_turned, dcol,
    first_col, last_col, inv_col, adj_col, sq_acc, gr_acc,
    piece, sib_piece, total, slices, scanned, landed, to_sib, from_sib, state,
    kgl_own, vgl_own, kl_own, vl_own, back_own, my_info, sib_info, chip_info, stat_out, stat_in,
    in_sem, sib_sem, up_send, up_recv, a_send, a_recv, b_send, b_recv,
    down_send, down_recv, stat_sem,
):
    tokens, width = q.shape
    heads = width // DH
    half = heads // 2
    chips = nctx // 2
    across = math.isqrt(chips)
    along = chips // across
    rows = half * DH // chips
    blocks = tokens // DH
    tiles = tokens // TILE
    me = lax.axis_index("ctx")
    z = lax.axis_index("head")
    chip = lax.div(me, 2)
    core = lax.rem(me, 2)
    sibling = me + 1 - 2 * core
    mine, other = core * half, (1 - core) * half
    here_y, here_x = lax.div(chip, across), lax.rem(chip, across)
    row_offsets = sorted(range(along), key=lambda d: -min(d, along - d))
    column_offsets = sorted(range(across), key=lambda d: -min(d, across - d))
    groups = [row_offsets[: along // 2], row_offsets[along // 2 :]]

    def cols(h):
        return pl.ds(pl.multiple_of(h * DH, DH), DH)

    def side(s):
        return pl.ds(pl.multiple_of(s * (width // 2), width // 2), width // 2)

    def slot(i):
        return pl.ds(pl.multiple_of(i * rows, rows), rows)

    def chip_at(offset):
        y = lax.rem(here_y + offset[0], along)
        x = lax.rem(here_x + offset[1], across)
        return y * across + x

    def head_at(d):
        return lax.rem(here_y + d, along)

    def to_chip(i):
        return {"ctx": 2 * i + core}

    chip_offsets = far_first(chips)
    head_offsets = sorted(range(1, nhead), key=lambda d: -min(d, nhead - d))

    def load(i, src, dst, s):
        return pltpu.make_async_copy(src.at[:, side(s)], dst.at[:, side(s)], in_sem.at[i])

    first_loads = [load(0, k_hbm, k, 1 - core), load(1, v_hbm, v, 1 - core)]
    docs_load = pltpu.make_async_copy(docs_hbm, docs, in_sem.at[2])
    own_loads = [load(3, k_hbm, k, core), load(4, v_hbm, v, core)]
    later_loads = [
        pltpu.make_async_copy(q_hbm, q, in_sem.at[5]),
        pltpu.make_async_copy(dy_hbm, dy, in_sem.at[6]),
        pltpu.make_async_copy(gain_hbm, gain, in_sem.at[7]),
    ]
    docs_load.start()
    for copy in first_loads:
        copy.start()

    barrier = pltpu.get_barrier_semaphore()

    def greet(device):
        pl.semaphore_signal(barrier, inc=1, device_id=device, device_id_type=MESH)

    for offset in chip_offsets:
        greet({"ctx": 2 * chip_at(offset)})
    for offset in head_offsets:
        greet({"ctx": 2 * chip, "head": lax.rem(z + offset, nhead)})
    greet({"ctx": sibling})
    for copy in own_loads + later_loads:
        copy.start()

    docs_load.wait()
    drow = docs[...].astype(F32)
    first_id = drow[:, 0:1]
    last_id = drow[:, tokens - 1 : tokens]
    my_info[0:1, :] = jnp.broadcast_to(first_id, (1, DH))
    my_info[1:2, :] = jnp.broadcast_to(last_id, (1, DH))
    for b in range(blocks):
        block = slice(b * DH, (b + 1) * DH)
        dcol[block, :] = jnp.broadcast_to(drow[:, block], (DH, DH)).T
    first_col[...] = equal(dcol[...], first_id)
    last_col[...] = equal(dcol[...], last_id).astype(BF16)

    def to_sibling(src, dst, send_sem, recv_sem):
        return pltpu.make_async_remote_copy(
            src_ref=src,
            dst_ref=dst,
            send_sem=send_sem,
            recv_sem=recv_sem,
            device_id={"ctx": sibling},
            device_id_type=MESH,
        )

    def push_up(g, d):
        at = cols(other + head_at(d))
        return to_sibling(
            piece.at[1, at, :], sib_piece.at[1, at, :], up_send.at[1], up_recv.at[1, g]
        )

    def up_heads(turn, g, first, last):
        at = slice(first * DH, last * DH)
        return to_sibling(
            piece.at[turn, at, :], sib_piece.at[turn, at, :],
            up_send.at[turn], up_recv.at[turn, g],
        )

    def push_down(turn, head):
        return to_sibling(
            to_sib.at[turn, cols(head), :], from_sib.at[turn, cols(head), :],
            down_send.at[turn], down_recv.at[turn, head],
        )

    def send_slice(src, dst, send_sem, recv_sem, device):
        pltpu.make_async_remote_copy(
            src_ref=src,
            dst_ref=dst,
            send_sem=send_sem,
            recv_sem=recv_sem,
            device_id=device,
            device_id_type=MESH,
        ).start()

    def sent_rows(turn):
        return slice(0, rows + 8) if turn == 0 else slice(0, rows)

    def slices_whole(turn, count):
        part = (slice(0, count), sent_rows(turn))
        return to_sibling(total.at[part], total.at[part], a_send.at[turn], a_recv.at[turn])

    def back_whole(turn, count, row):
        part = (turn, slice(0, count * rows))
        return to_sibling(
            scanned.at[part], landed.at[part], b_send.at[turn], b_recv.at[turn, row]
        )

    def orders(turn):
        return (0, 1, 2, 3) if turn == 0 else (3, 2, 1, 0)

    def is_near(turn):
        return jnp.full((1, DH), core if turn == 0 else 1 - core, jnp.int32) == 0

    def ids_of(row):
        return chip_info[row : row + 1, :]

    def add_up(turn, head, place):
        _, near_last, _, far_last = orders(turn)
        joined = equal(ids_of(near_last), ids_of(far_last))
        own_share = jnp.where(is_near(turn), joined, 1.0)
        sib_share = jnp.where(is_near(turn), 1.0, joined)
        for x in range(across):
            part = pl.ds(pl.multiple_of(head * DH + x * rows, rows), rows)
            total[place + x, 0:rows, :] = (
                piece[turn, part, :] * own_share + sib_piece[turn, part, :] * sib_share
            )

    def ascend_forward():
        @pl.when(core == 1)
        def _():
            pl.semaphore_wait(barrier, 1)
            sib_ids.start()
            up_heads(0, 0, 0, heads).start()

        @pl.when(core == 0)
        def _():
            sib_ids.wait_recv()
            chip_info[0:2, :] = my_info[0:2, :]
            chip_info[2:4, :] = sib_info[0:2, :]
            up_heads(0, 0, 0, heads).wait_recv()
            for head in range(heads):
                add_up(0, head, head * across)
            for i in range(2 * chips):
                total[i, rows : rows + 8, :] = chip_info[...]
            pl.semaphore_wait(barrier, 1 + 2 * (chips - 1) + 2 * (nhead - 1))
            for offset in chip_offsets:
                i = chip_at(offset)
                for a in range(2):
                    send_slice(
                        total.at[a * chips + i], slices.at[0, chip],
                        a_send.at[0], a_recv.at[0], {"ctx": 2 * i + a},
                    )
            send_slice(
                total.at[chips + chip], slices.at[0, chip],
                a_send.at[0], a_recv.at[0], {"ctx": sibling},
            )
            up_heads(0, 0, half, heads).start()
            slices[0, chip] = total[chip]

    def ascend_backward():
        for g, group in enumerate(groups):
            up_heads(1, g, 0, len(group)).wait_recv()
            for d in group:
                head = head_at(d)
                add_up(1, mine + head, 2 * chips + head * across)
            for offset in chip_offsets:
                if offset[0] in group:
                    i = chip_at(offset)
                    send_slice(
                        total.at[2 * chips + i, sent_rows(1)], slices.at[1, chip, sent_rows(1)],
                        a_send.at[1], a_recv.at[1], to_chip(i),
                    )
        slices[1, chip] = total[2 * chips + chip]

    def scan(turn):
        near_first, _, _, far_last = orders(turn)
        if turn == 0:

            @pl.when(core == 0)
            def _():
                slices_whole(0, chips - 1).wait_recv()

            @pl.when(core == 1)
            def _():
                slices_whole(0, chips).wait_recv()
                up_heads(0, 0, half, heads).wait_recv()
                chip_info[...] = slices[0, chip, rows : rows + 8, :]

        else:
            slices_whole(1, chips - 1).wait_recv()
        running = jnp.zeros((rows, DH), F32)
        before = jnp.full((1, DH), -1.0, F32)
        for j in range(chips):
            i = j if turn == 0 else chips - 1 - j
            ids = slices[0, i, rows : rows + 8, :]
            enters = ids[near_first : near_first + 1, :]
            leaves = ids[far_last : far_last + 1, :]
            here = slice(i * rows, (i + 1) * rows)
            scanned[turn, here, :] = running * equal(before, enters)
            running = slices[turn, i, 0:rows, :] + running * equal(before, leaves)
            before = leaves
        for offset in chip_offsets:
            i = chip_at(offset)
            send_slice(
                scanned.at[turn, slot(i), :], landed.at[turn, slot(chip), :],
                b_send.at[turn], b_recv.at[turn, here_y], to_chip(i),
            )
        landed[turn, slot(chip), :] = scanned[turn, slot(chip), :]

    def descend(turn, into, then):
        near_first, near_last, far_first, _ = orders(turn)
        next_to = equal(ids_of(near_last), ids_of(far_first))
        through = equal(ids_of(near_first), ids_of(far_first))
        near = is_near(turn)
        own_enter = jnp.where(near, 1.0, through)
        own_sib = jnp.where(near, 0.0, next_to)
        sib_enter = jnp.where(near, through, 1.0)
        sib_own = jnp.where(near, next_to, 0.0)
        for d in reversed(row_offsets):
            head = head_at(d)
            at = cols(head)
            back_whole(turn, across - (d == 0), head).wait_recv()
            to_sib[turn, at, :] = (
                landed[turn, at, :] * sib_enter + piece[turn, cols(mine + head), :] * sib_own
            )
            push_down(turn, head).start()
            beyond = sib_piece[turn, cols(mine + head), :]
            into(head, landed[turn, at, :] * own_enter + beyond * own_sib)
            then(head)

    sib_ids = to_sibling(my_info, sib_info, sib_sem.at[0], sib_sem.at[1])

    def settle(turn):
        whole = to_sibling(
            to_sib.at[turn], from_sib.at[turn], down_send.at[turn], down_recv.at[turn, 0]
        )
        whole.wait_send()
        back_whole(turn, chips - 1, 0).wait_send()
        if turn == 0:

            @pl.when(core == 0)
            def _():
                up_heads(0, 0, half, heads).wait_send()
                slices_whole(0, 2 * chips - 1).wait_send()

            @pl.when(core == 1)
            def _():
                up_heads(0, 0, 0, heads).wait_send()
                sib_ids.wait_send()

        else:
            up_heads(1, 0, 0, half).wait_send()
            slices_whole(1, chips - 1).wait_send()

    def make_piece(h):
        piece[0, cols(h), :] = tn(k[:, cols(h)] * last_col[...], v[:, cols(h)])

    for copy in first_loads:
        copy.wait()
    for j in range(half):
        make_piece(other + j)
    for copy in own_loads:
        copy.wait()
    for j in range(half):
        make_piece(mine + j)
    ascend_forward()

    later = lax.broadcasted_iota(jnp.int32, (tokens, DH), 0)
    for b in range(blocks):
        block = slice(b * DH, (b + 1) * DH)
        earlier = lax.broadcasted_iota(jnp.int32, (tokens, DH), 1) + b * DH
        ids = jnp.broadcast_to(drow[:, block], (tokens, DH))
        same[:, block] = jnp.where((dcol[...] == ids) & (later >= earlier), 1.0, 0.0).astype(BF16)
    for copy in later_loads:
        copy.wait()

    def local_forward(h, carry):
        firsts = q[:, cols(h)] * first_col[...].astype(BF16)
        qf[:, cols(h)] = firsts
        qf_turned[cols(h), :] = firsts.T
        scaled[:, cols(h)] = gain[:, cols(h)] * dy[:, cols(h)].astype(F32)
        for r in range(tiles):
            here, upto = slice(r * TILE, (r + 1) * TILE), slice(0, (r + 1) * TILE)
            scores = nt(q[here, cols(h)], k[upto, cols(h)])
            masked = scores.astype(BF16) * same[here, upto]
            weights[h, here, upto] = masked
            att[here, cols(h)] = nn(masked, v[upto, cols(h)])
        return carry

    lax.fori_loop(0, heads, local_forward, 0, unroll=2)
    scan(0)

    def attend(h):
        whole = att[:, cols(h)] + nn(qf[:, cols(h)], state[cols(h), :])
        att[:, cols(h)] = whole
        squares, grads = whole * whole, scaled[:, cols(h)] * whole
        sq_acc[...] += squares
        gr_acc[...] += grads

    def enter(head, block):
        state[cols(mine + head), :] = block.astype(BF16)

    sq_acc[...] = jnp.zeros_like(sq_acc)
    gr_acc[...] = jnp.zeros_like(gr_acc)
    descend(0, enter, lambda head: attend(mine + head))
    arrivals = [head_at(d) for d in reversed(row_offsets)]
    for group in (arrivals[:-1], arrivals[-1:]):
        for head in group:
            push_down(0, head).wait_recv()
        for head in group:
            state[cols(other + head), :] = from_sib[0, cols(head), :].astype(BF16)
            attend(other + head)
    square_sums, grad_sums = row_sums(sq_acc[...]), row_sums(gr_acc[...])
    for b in range(blocks):
        block = slice(b * DH, (b + 1) * DH)
        stat_out[b : b + 1, :] = square_sums[:, block]
        stat_out[blocks + b : blocks + b + 1, :] = grad_sums[:, block]
    for offset in head_offsets:
        pltpu.make_async_remote_copy(
            src_ref=stat_out,
            dst_ref=stat_in.at[z],
            send_sem=stat_sem.at[0],
            recv_sem=stat_sem.at[1],
            device_id={"head": lax.rem(z + offset, nhead)},
            device_id_type=MESH,
        ).start()
    stat_in[z] = stat_out[...]
    settle(0)
    stat_whole = pltpu.make_async_remote_copy(
        src_ref=stat_in.at[0 : nhead - 1],
        dst_ref=stat_in.at[0 : nhead - 1],
        send_sem=stat_sem.at[0],
        recv_sem=stat_sem.at[1],
        device_id={"ctx": sibling},
        device_id_type=MESH,
    )
    stat_whole.wait_recv()
    sums = stat_in[0]
    for at in range(1, nhead):
        sums = sums + stat_in[at]
    means = sums / (width * nhead)
    inv = lax.rsqrt(means[0:blocks, :] + epsilon)
    factor = inv * inv * inv * means[blocks : 2 * blocks, :]
    turned = jnp.concatenate([inv, factor] * (DH // (2 * blocks)), axis=0).T
    for b in range(blocks):
        block = slice(b * DH, (b + 1) * DH)
        inv_col[block, :] = jnp.broadcast_to(turned[:, b : b + 1], (DH, DH))
        adj_col[block, :] = jnp.broadcast_to(turned[:, blocks + b : blocks + b + 1], (DH, DH))

    def adjoint(h):
        grads = (inv_col[...] * scaled[:, cols(h)] - att[:, cols(h)] * adj_col[...]).astype(BF16)
        oa[:, cols(h)] = grads
        piece[1, cols(h), :] = nn(qf_turned[cols(h), :], grads)

    for g, group in enumerate(groups):
        for d in group:
            adjoint(other + head_at(d))
        for d in group:
            push_up(g, d).start()
    for j in range(half):
        adjoint(mine + j)
    ascend_backward()

    def local_backward(j, carry, base, kgl, vgl, kl, vl):
        h = base + j
        kl[:, cols(j)] = k[:, cols(h)] * last_col[...]
        vl[:, cols(j)] = v[:, cols(h)] * last_col[...]
        grads = oa[:, cols(h)]
        stepped = nt(grads, state[cols(h), :]) * first_col[...]
        for r in range(tiles):
            here, upto = slice(r * TILE, (r + 1) * TILE), slice(0, (r + 1) * TILE)
            scores = nt(grads[here], v[upto, cols(h)])
            masked = scores.astype(BF16) * same[here, upto]
            adj[here, upto] = masked
            qg[here, cols(h)] = (nn(masked, k[upto, cols(h)]) + stepped[here]).astype(BF16)
        for r in range(tiles):
            here, onward = slice(r * TILE, (r + 1) * TILE), slice(r * TILE, tokens)
            kgl[here, cols(j)] = tn(adj[onward, here], q[onward, cols(h)])
            vgl[here, cols(j)] = tn(weights[h, onward, here], grads[onward])
        normed[:, cols(h)] = (gain[:, cols(h)] * att[:, cols(h)] * inv_col[...]).astype(BF16)
        return carry

    own_half = functools.partial(
        local_backward, base=mine, kgl=kgl_own, vgl=vgl_own, kl=kl_own, vl=vl_own
    )
    other_half = functools.partial(
        local_backward, base=other, kgl=kgl_other, vgl=vgl_other, kl=kl_other, vl=vl_other
    )
    lax.fori_loop(0, half, own_half, 0, unroll=2)
    scan(1)
    lax.fori_loop(0, half, other_half, 0, unroll=2)

    def enter_back(head, block):
        back_own[cols(head), :] = block.astype(BF16)

    descend(1, enter_back, lambda head: None)
    last_products(kg_own, vg_own, kgl_own, vgl_own, kl_own, vl_own, back_own)
    stat_whole.wait_send()
    for head in arrivals:
        push_down(1, head).wait_recv()
    back_other[...] = from_sib[1].astype(BF16)
    settle(1)


def last_products(kg, vg, kgl, vgl, kl, vl, back_state):
    for h in range(kg.shape[1] // DH):
        at = slice(h * DH, (h + 1) * DH)
        back = back_state[at, :]
        kg[:, at] = (kgl[:, at] + nt(vl[:, at], back)).astype(BF16)
        vg[:, at] = (vgl[:, at] + nn(kl[:, at], back)).astype(BF16)


def finish(
    normed, qg, kg_own, vg_own, kgl_other, vgl_other, kl_other, vl_other, back_other,
    normed_hbm, qg_hbm, kg_hbm, vg_hbm,
    kg_other, vg_other, out_sem,
):
    core = lax.rem(lax.axis_index("ctx"), 2)
    part = kg_other.shape[1]

    def side(s):
        return pl.ds(pl.multiple_of(s * part, part), part)

    stores = [
        pltpu.make_async_copy(normed, normed_hbm, out_sem.at[0]),
        pltpu.make_async_copy(qg, qg_hbm, out_sem.at[1]),
        pltpu.make_async_copy(kg_own, kg_hbm.at[:, side(core)], out_sem.at[2]),
        pltpu.make_async_copy(vg_own, vg_hbm.at[:, side(core)], out_sem.at[3]),
    ]
    for copy in stores:
        copy.start()
    last_products(kg_other, vg_other, kgl_other, vgl_other, kl_other, vl_other, back_other)
    for i, (src, dst) in enumerate(((kg_other, kg_hbm), (vg_other, vg_hbm))):
        copy = pltpu.make_async_copy(src, dst.at[:, side(1 - core)], out_sem.at[4 + i])
        copy.start()
        stores.append(copy)
    for copy in stores:
        copy.wait()


def body(nctx, nhead, query_rows, key_rows, value_rows, out_grad, norm_gain, doc_ids):
    tokens, width = query_rows.shape
    heads = width // DH
    half = heads // 2
    chips = nctx // 2
    rows = half * DH // chips
    blocks = tokens // DH
    grid = (tokens, width)
    half_grid = (tokens, width // 2)
    dma = pltpu.SemaphoreType.DMA
    scratch = [
        *[pltpu.VMEM(grid, BF16)] * 6,
        *[pltpu.VMEM(grid, F32)] * 2,
        pltpu.VMEM((heads, tokens, tokens), BF16),
        pltpu.VMEM((tokens, tokens), BF16),
        pltpu.VMEM((tokens, tokens), BF16),
        pltpu.VMEM((1, width), F32),
        pltpu.VMEM((1, tokens), jnp.int32),
        pltpu.VMEM((heads * DH, tokens), BF16),
        *[pltpu.VMEM((tokens, DH), F32)] * 2,
        pltpu.VMEM((tokens, DH), BF16),
        *[pltpu.VMEM((tokens, DH), F32)] * 4,
        pltpu.VMEM((2, heads * DH, DH), F32),
        pltpu.VMEM((2, heads * DH, DH), F32),
        pltpu.VMEM((3 * chips, rows + 8, DH), F32),
        pltpu.VMEM((2, chips, rows + 8, DH), F32),
        *[pltpu.VMEM((2, half * DH, DH), F32)] * 4,
        pltpu.VMEM((heads * DH, DH), BF16),
        *[pltpu.VMEM(half_grid, F32)] * 2,
        *[pltpu.VMEM(half_grid, BF16)] * 2,
        pltpu.VMEM((half * DH, DH), BF16),
        *[pltpu.VMEM((8, DH), F32)] * 3,
        pltpu.VMEM((2 * blocks, DH), F32),
        pltpu.VMEM((nhead, 2 * blocks, DH), F32),
        dma((8,)),
        *[dma((2,))] * 2,
        dma((2, 2)),
        *[dma((2,))] * 3,
        dma((2, half)),
        dma((2,)),
        dma((2, half)),
        dma((2,)),
    ]
    arrays = (
        query_rows, key_rows, value_rows, out_grad,
        norm_gain.reshape(1, width), doc_ids.reshape(1, tokens),
    )
    anywhere = pl.BlockSpec(memory_space=pl.ANY)
    in_hbm = pl.BlockSpec(memory_space=pltpu.HBM)
    in_vmem = pl.BlockSpec(memory_space=pltpu.VMEM)
    parts = pl.pallas_call(
        functools.partial(kernel, nctx, nhead),
        out_shape=[
            *[jax.ShapeDtypeStruct(grid, BF16)] * 2,
            *[jax.ShapeDtypeStruct(half_grid, BF16)] * 2,
            *[jax.ShapeDtypeStruct(half_grid, F32)] * 2,
            *[jax.ShapeDtypeStruct(half_grid, BF16)] * 2,
            jax.ShapeDtypeStruct((half * DH, DH), BF16),
        ],
        in_specs=[in_hbm] * 6,
        out_specs=[in_vmem] * 9,
        scratch_shapes=scratch,
        compiler_params=pltpu.CompilerParams(
            collective_id=0, has_side_effects=True, vmem_limit_bytes=44 * 2**20
        ),
        name="attend",
    )(*[pltpu.with_memory_space_constraint(array, pltpu.HBM) for array in arrays])
    return pl.pallas_call(
        finish,
        out_shape=[jax.ShapeDtypeStruct(grid, BF16)] * 4,
        in_specs=[in_vmem] * 9,
        out_specs=[anywhere] * 4,
        scratch_shapes=[*[pltpu.VMEM(half_grid, BF16)] * 2, dma((6,))],
        compiler_params=pltpu.CompilerParams(vmem_limit_bytes=16 * 2**20),
        name="finish",
    )(*parts)


def solution(mesh):
    nctx, nhead = mesh.shape["ctx"], mesh.shape["head"]
    placed = (
        P("ctx", "head"),
        P("ctx", "head"),
        P("ctx", "head"),
        P("ctx", "head"),
        P("head"),
        P("ctx"),
    )
    return jax.shard_map(
        functools.partial(body, nctx, nhead),
        mesh=mesh,
        in_specs=placed,
        out_specs=(P("ctx", "head"), P("ctx", "head"), P("ctx", "head"), P("ctx", "head")),
        check_vma=False,
    )
```

```python
import functools
import math

import jax
import jax.numpy as jnp
from jax import lax
from jax.experimental import pallas as pl
from jax.experimental.pallas import tpu as pltpu
from jax.sharding import PartitionSpec as P

DH = 128
TILE = 256
epsilon = 1e-05
MESH = pl.DeviceIdType.MESH
F32 = jnp.float32
BF16 = jnp.bfloat16


def nn(a, b):
    return lax.dot_general(a, b, (((1,), (0,)), ((), ())), preferred_element_type=F32)


def nt(a, b):
    return lax.dot_general(a, b, (((1,), (1,)), ((), ())), preferred_element_type=F32)


def tn(a, b):
    return lax.dot_general(a, b, (((0,), (0,)), ((), ())), preferred_element_type=F32)


def equal(a, b):
    return jnp.where(a == b, 1.0, 0.0).astype(F32)


def row_sums(values):
    ones = jnp.ones((8, DH), BF16)
    high = values.astype(BF16)
    low = (values - high.astype(F32)).astype(BF16)
    return (nt(ones, high) + nt(ones, low))[0:1, :]


def far_first(chips):
    across = math.isqrt(chips)
    along = chips // across

    def hops(offset):
        dy, dx = offset
        return min(dy, along - dy) + min(dx, across - dx)

    offsets = [(dy, dx) for dy in range(along) for dx in range(across) if dy + dx > 0]
    return sorted(offsets, key=hops, reverse=True)


def kernel(
    nctx, nhead,
    q_hbm, k_hbm, v_hbm, dy_hbm, gain_hbm, docs_hbm,
    normed, qg, kgl0, kgl1, vgl0, vgl1, kl, vl, back_state,
    q, k, v, dy, qf, oa, att, scaled, weights, adj, same, gain, docs, qf_turned, dcol,
    first_col, last_col, inv_col, adj_col, sq_acc, gr_acc,
    piece, sib_piece, total, slices, scanned, landed, to_sib, from_sib, state,
    my_info, sib_info, chip_info, stat_out, stat_in, stat_sum,
    qf_wide, qf_in, att_sib, scaled_sib, qf_sib, turned_sib, state_sib,
    sq_sib, gr_sib, inv_sib, adj_sib,
    in_sem, sib_sem, up_send, up_recv, a_send, a_recv, b_send, b_recv,
    down_send, down_recv, stat_sem, swap_send, swap_recv,
):
    tokens, width = q.shape
    heads = width // DH
    half = heads // 2
    chips = nctx // 2
    across = math.isqrt(chips)
    along = chips // across
    rows = half * DH // chips
    blocks = tokens // DH
    tiles = tokens // TILE
    me = lax.axis_index("ctx")
    z = lax.axis_index("head")
    chip = lax.div(me, 2)
    core = lax.rem(me, 2)
    sibling = me + 1 - 2 * core
    mine, other = core * half, (1 - core) * half
    here_y, here_x = lax.div(chip, across), lax.rem(chip, across)
    row_offsets = sorted(range(along), key=lambda d: -min(d, along - d))
    column_offsets = sorted(range(across), key=lambda d: -min(d, across - d))

    def cols(h):
        return pl.ds(pl.multiple_of(h * DH, DH), DH)

    def side(s):
        return pl.ds(pl.multiple_of(s * (width // 2), width // 2), width // 2)

    def slot(i):
        return pl.ds(pl.multiple_of(i * rows, rows), rows)

    def chip_at(offset):
        y = lax.rem(here_y + offset[0], along)
        x = lax.rem(here_x + offset[1], across)
        return y * across + x

    def head_at(d):
        return lax.rem(here_y + d, along)

    def to_chip(i):
        return {"ctx": 2 * i + core}

    chip_offsets = far_first(chips)
    head_offsets = sorted(range(1, nhead), key=lambda d: -min(d, nhead - d))

    def load(i, src, dst, s):
        return pltpu.make_async_copy(src.at[:, side(s)], dst.at[:, side(s)], in_sem.at[i])

    first_loads = [load(0, k_hbm, k, 1 - core), load(1, v_hbm, v, 1 - core)]
    docs_load = pltpu.make_async_copy(docs_hbm, docs, in_sem.at[2])
    own_loads = [load(3, k_hbm, k, core), load(4, v_hbm, v, core)]
    later_loads = [
        pltpu.make_async_copy(q_hbm, q, in_sem.at[5]),
        pltpu.make_async_copy(dy_hbm, dy, in_sem.at[6]),
        pltpu.make_async_copy(gain_hbm, gain, in_sem.at[7]),
    ]
    docs_load.start()
    for copy in first_loads + own_loads:
        copy.start()

    barrier = pltpu.get_barrier_semaphore()

    def greet(device):
        pl.semaphore_signal(barrier, inc=1, device_id=device, device_id_type=MESH)

    for offset in chip_offsets:
        greet({"ctx": 2 * chip_at(offset)})
    for offset in head_offsets:
        greet({"ctx": 2 * chip, "head": lax.rem(z + offset, nhead)})
    greet({"ctx": sibling})
    for copy in later_loads:
        copy.start()

    docs_load.wait()
    drow = docs[...].astype(F32)
    first_id = drow[:, 0:1]
    last_id = drow[:, tokens - 1 : tokens]
    my_info[0:1, :] = jnp.broadcast_to(first_id, (1, DH))
    my_info[1:2, :] = jnp.broadcast_to(last_id, (1, DH))
    for b in range(blocks):
        block = slice(b * DH, (b + 1) * DH)
        dcol[block, :] = jnp.broadcast_to(drow[:, block], (DH, DH)).T
    first_col[...] = equal(dcol[...], first_id)
    last_col[...] = equal(dcol[...], last_id).astype(BF16)

    def to_sibling(src, dst, send_sem, recv_sem):
        return pltpu.make_async_remote_copy(
            src_ref=src,
            dst_ref=dst,
            send_sem=send_sem,
            recv_sem=recv_sem,
            device_id={"ctx": sibling},
            device_id_type=MESH,
        )

    def up_heads(turn, g, first, last):
        at = slice(first * DH, last * DH)
        return to_sibling(
            piece.at[turn, at, :], sib_piece.at[turn, at, :],
            up_send.at[turn], up_recv.at[turn, g],
        )

    def push_down(turn, head):
        return to_sibling(
            to_sib.at[turn, cols(head), :], from_sib.at[turn, cols(head), :],
            down_send.at[turn], down_recv.at[turn, head],
        )

    def send_slice(src, dst, send_sem, recv_sem, device):
        pltpu.make_async_remote_copy(
            src_ref=src,
            dst_ref=dst,
            send_sem=send_sem,
            recv_sem=recv_sem,
            device_id=device,
            device_id_type=MESH,
        ).start()

    def sent_rows(turn):
        return slice(0, rows + 8) if turn == 0 else slice(0, rows)

    def slices_whole(turn, count):
        part = (slice(0, count), sent_rows(turn))
        return to_sibling(total.at[part], total.at[part], a_send.at[turn], a_recv.at[turn])

    def back_whole(turn, count, row):
        part = (turn, slice(0, count * rows))
        return to_sibling(
            scanned.at[part], landed.at[part], b_send.at[turn], b_recv.at[turn, row]
        )

    def swap(n):
        src, dst = (
            (scaled.at[:, side(1 - core)], scaled_sib),
            (qf_wide, qf_in),
            (att.at[:, side(1 - core)], att_sib),
        )[n]
        return to_sibling(src, dst, swap_send.at[n], swap_recv.at[n])

    def orders(turn):
        return (0, 1, 2, 3) if turn == 0 else (3, 2, 1, 0)

    def is_near(turn):
        return jnp.full((1, DH), core if turn == 0 else 1 - core, jnp.int32) == 0

    def ids_of(row):
        return chip_info[row : row + 1, :]

    def add_up(turn, head, place):
        _, near_last, _, far_last = orders(turn)
        joined = equal(ids_of(near_last), ids_of(far_last))
        own_share = jnp.where(is_near(turn), joined, 1.0)
        sib_share = jnp.where(is_near(turn), 1.0, joined)
        for x in range(across):
            part = pl.ds(pl.multiple_of(head * DH + x * rows, rows), rows)
            total[place + x, 0:rows, :] = (
                piece[turn, part, :] * own_share + sib_piece[turn, part, :] * sib_share
            )

    def ascend_forward():
        for copy in first_loads:
            copy.wait()

        @pl.when(core == 1)
        def _():
            for h in range(half):
                make_piece(h)
            pl.semaphore_wait(barrier, 1)
            sib_ids.start()
            up_heads(0, 0, 0, half).start()
            for copy in own_loads:
                copy.wait()
            for h in range(half, heads):
                make_piece(h)
            up_heads(0, 1, half, heads).start()

        @pl.when(core == 0)
        def _():
            for copy in own_loads:
                copy.wait()
            for h in range(heads):
                make_piece(h)
            sib_ids.wait_recv()
            chip_info[0:2, :] = my_info[0:2, :]
            chip_info[2:4, :] = sib_info[0:2, :]
            up_heads(0, 0, 0, half).wait_recv()
            for head in range(half):
                add_up(0, head, head * across)
            up_heads(0, 1, half, heads).wait_recv()
            for head in range(half, heads):
                add_up(0, head, head * across)
            for i in range(2 * chips):
                total[i, rows : rows + 8, :] = chip_info[...]
            pl.semaphore_wait(barrier, 1 + 2 * (chips - 1) + 2 * (nhead - 1))
            for offset in chip_offsets:
                i = chip_at(offset)
                for a in range(2):
                    send_slice(
                        total.at[a * chips + i], slices.at[0, chip],
                        a_send.at[0], a_recv.at[0], {"ctx": 2 * i + a},
                    )
            send_slice(
                total.at[chips + chip], slices.at[0, chip],
                a_send.at[0], a_recv.at[0], {"ctx": sibling},
            )
            up_heads(0, 0, half, heads).start()
            slices[0, chip] = total[chip]

    def ascend_backward():
        for head in range(half):
            add_up(1, mine + head, 2 * chips + head * across)
        for offset in chip_offsets:
            i = chip_at(offset)
            send_slice(
                total.at[2 * chips + i, sent_rows(1)], slices.at[1, chip, sent_rows(1)],
                a_send.at[1], a_recv.at[1], to_chip(i),
            )
        slices[1, chip] = total[2 * chips + chip]

    def scan(turn):
        near_first, _, _, far_last = orders(turn)
        if turn == 0:

            @pl.when(core == 0)
            def _():
                slices_whole(0, chips - 1).wait_recv()

            @pl.when(core == 1)
            def _():
                slices_whole(0, chips).wait_recv()
                up_heads(0, 0, half, heads).wait_recv()
                chip_info[...] = slices[0, chip, rows : rows + 8, :]

        else:
            slices_whole(1, chips - 1).wait_recv()
        running = jnp.zeros((rows, DH), F32)
        before = jnp.full((1, DH), -1.0, F32)
        for j in range(chips):
            i = j if turn == 0 else chips - 1 - j
            ids = slices[0, i, rows : rows + 8, :]
            enters = ids[near_first : near_first + 1, :]
            leaves = ids[far_last : far_last + 1, :]
            here = slice(i * rows, (i + 1) * rows)
            scanned[turn, here, :] = running * equal(before, enters)
            running = slices[turn, i, 0:rows, :] + running * equal(before, leaves)
            before = leaves
        for offset in chip_offsets:
            i = chip_at(offset)
            send_slice(
                scanned.at[turn, slot(i), :], landed.at[turn, slot(chip), :],
                b_send.at[turn], b_recv.at[turn, here_y], to_chip(i),
            )
        landed[turn, slot(chip), :] = scanned[turn, slot(chip), :]

    def descend(turn, into):
        near_first, near_last, far_first, _ = orders(turn)
        next_to = equal(ids_of(near_last), ids_of(far_first))
        through = equal(ids_of(near_first), ids_of(far_first))
        near = is_near(turn)
        own_enter = jnp.where(near, 1.0, through)
        own_sib = jnp.where(near, 0.0, next_to)
        sib_enter = jnp.where(near, through, 1.0)
        sib_own = jnp.where(near, next_to, 0.0)
        for d in reversed(row_offsets):
            head = head_at(d)
            at = cols(head)
            back_whole(turn, across - (d == 0), head).wait_recv()
            to_sib[turn, at, :] = (
                landed[turn, at, :] * sib_enter + piece[turn, cols(mine + head), :] * sib_own
            )
            push_down(turn, head).start()
            beyond = sib_piece[turn, cols(mine + head), :]
            into(head, landed[turn, at, :] * own_enter + beyond * own_sib)

    sib_ids = to_sibling(my_info, sib_info, sib_sem.at[0], sib_sem.at[1])

    def settle(turn):
        whole = to_sibling(
            to_sib.at[turn], from_sib.at[turn], down_send.at[turn], down_recv.at[turn, 0]
        )
        whole.wait_send()
        back_whole(turn, chips - 1, 0).wait_send()
        if turn == 0:

            @pl.when(core == 0)
            def _():
                up_heads(0, 0, half, heads).wait_send()
                slices_whole(0, 2 * chips - 1).wait_send()

            @pl.when(core == 1)
            def _():
                up_heads(0, 0, 0, heads).wait_send()
                sib_ids.wait_send()

            for n in range(3):
                swap(n).wait_send()
        else:
            slices_whole(1, chips - 1).wait_send()

    def make_piece(h):
        piece[0, cols(h), :] = tn(k[:, cols(h)] * last_col[...], v[:, cols(h)])

    ascend_forward()

    later = lax.broadcasted_iota(jnp.int32, (tokens, DH), 0)
    for b in range(blocks):
        block = slice(b * DH, (b + 1) * DH)
        earlier = lax.broadcasted_iota(jnp.int32, (tokens, DH), 1) + b * DH
        ids = jnp.broadcast_to(drow[:, block], (tokens, DH))
        same[:, block] = jnp.where((dcol[...] == ids) & (later >= earlier), 1.0, 0.0).astype(BF16)
    for copy in later_loads:
        copy.wait()

    def prepare(j, carry, base):
        h = base + j
        qf[:, cols(h)] = q[:, cols(h)] * first_col[...].astype(BF16)
        scaled[:, cols(h)] = gain[:, cols(h)] * dy[:, cols(h)].astype(F32)
        return carry

    def widen(j, carry):
        qf_wide[:, cols(j)] = qf[:, cols(other + j)].astype(F32)
        return carry

    lax.fori_loop(0, half, functools.partial(prepare, base=other), 0)
    lax.fori_loop(0, half, widen, 0)
    swap(0).start()
    swap(1).start()

    def local_forward(j, carry, base):
        h = base + j
        for r in range(tiles):
            here, upto = slice(r * TILE, (r + 1) * TILE), slice(0, (r + 1) * TILE)
            scores = nt(q[here, cols(h)], k[upto, cols(h)])
            masked = scores.astype(BF16) * same[here, upto]
            weights[h, here, upto] = masked
            att[here, cols(h)] = nn(masked, v[upto, cols(h)])
        return carry

    lax.fori_loop(0, half, functools.partial(local_forward, base=other), 0, unroll=2)
    swap(2).start()
    scan(0)
    lax.fori_loop(0, half, functools.partial(prepare, base=mine), 0)
    lax.fori_loop(0, half, functools.partial(local_forward, base=mine), 0, unroll=2)
    for n in range(3):
        swap(n).wait_recv()

    def turn_queries(j, carry):
        queries = qf_in[:, cols(j)].astype(BF16)
        qf_sib[:, cols(j)] = queries
        turned_sib[cols(j), :] = queries.T
        qf_turned[cols(j), :] = qf[:, cols(mine + j)].T
        return carry

    lax.fori_loop(0, half, turn_queries, 0)

    def enter(head, block):
        state[cols(mine + head), :] = block.astype(BF16)

    descend(0, enter)
    sq_acc[...] = jnp.zeros_like(sq_acc)
    gr_acc[...] = jnp.zeros_like(gr_acc)
    sq_sib[...] = jnp.zeros_like(sq_sib)
    gr_sib[...] = jnp.zeros_like(gr_sib)
    state_sib[...] = to_sib[0].astype(BF16)
    for j in range(half):
        whole = att[:, cols(mine + j)] + nn(qf[:, cols(mine + j)], state[cols(mine + j), :])
        att[:, cols(mine + j)] = whole
        sq_acc[...] += whole * whole
        gr_acc[...] += scaled[:, cols(mine + j)] * whole
    for j in range(half):
        whole = att_sib[:, cols(j)] + nn(qf_sib[:, cols(j)], state_sib[cols(j), :])
        att_sib[:, cols(j)] = whole
        sq_sib[...] += whole * whole
        gr_sib[...] += scaled_sib[:, cols(j)] * whole
    for at, squares, grads in ((core, sq_acc, gr_acc), (1 - core, sq_sib, gr_sib)):
        square_sums, grad_sums = row_sums(squares[...]), row_sums(grads[...])
        for b in range(blocks):
            block = slice(b * DH, (b + 1) * DH)
            stat_out[at, b : b + 1, :] = square_sums[:, block]
            stat_out[at, blocks + b : blocks + b + 1, :] = grad_sums[:, block]

    def send_stat(device):
        pltpu.make_async_remote_copy(
            src_ref=stat_out,
            dst_ref=stat_in.at[2 * z + core],
            send_sem=stat_sem.at[0],
            recv_sem=stat_sem.at[1],
            device_id=device,
            device_id_type=MESH,
        ).start()

    for offset in head_offsets:
        for a in (core, 1 - core):
            send_stat({"ctx": 2 * chip + a, "head": lax.rem(z + offset, nhead)})
    send_stat({"ctx": sibling})
    stat_in[2 * z + core] = stat_out[...]
    settle(0)
    for d in reversed(row_offsets):
        head = head_at(d)
        push_down(0, head).wait_recv()
        state[cols(other + head), :] = from_sib[0, cols(head), :].astype(BF16)
    for j in range(half):
        att[:, cols(other + j)] += nn(qf[:, cols(other + j)], state[cols(other + j), :])
    stat_whole = to_sibling(
        stat_in.at[0 : 2 * nhead - 1], stat_in.at[0 : 2 * nhead - 1],
        stat_sem.at[0], stat_sem.at[1],
    )
    stat_whole.wait_recv()
    sums = stat_in[0]
    for at in range(1, 2 * nhead):
        sums = sums + stat_in[at]
    stat_sum[...] = sums / (width * nhead)
    for at, inv_to, adj_to in ((core, inv_col, adj_col), (1 - core, inv_sib, adj_sib)):
        means = stat_sum[at]
        inv = lax.rsqrt(means[0:blocks, :] + epsilon)
        factor = inv * inv * inv * means[blocks : 2 * blocks, :]
        turned = jnp.concatenate([inv, factor] * (DH // (2 * blocks)), axis=0).T
        for b in range(blocks):
            block = slice(b * DH, (b + 1) * DH)
            inv_to[block, :] = jnp.broadcast_to(turned[:, b : b + 1], (DH, DH))
            adj_to[block, :] = jnp.broadcast_to(
                turned[:, blocks + b : blocks + b + 1], (DH, DH)
            )

    def adjoint(h):
        return (inv_col[...] * scaled[:, cols(h)] - att[:, cols(h)] * adj_col[...]).astype(BF16)

    for j in range(half):
        grads = adjoint(mine + j)
        oa[:, cols(mine + j)] = grads
        piece[1, cols(mine + j), :] = nn(qf_turned[cols(j), :], grads)
    for j in range(half):
        grads = (
            inv_sib[...] * scaled_sib[:, cols(j)] - att_sib[:, cols(j)] * adj_sib[...]
        ).astype(BF16)
        sib_piece[1, cols(mine + j), :] = nn(turned_sib[cols(j), :], grads)
    ascend_backward()
    for j in range(half):
        oa[:, cols(other + j)] = adjoint(other + j)

    def local_backward(j, carry, base, kgl, vgl):
        h = base + j
        kl[:, cols(h)] = k[:, cols(h)] * last_col[...]
        vl[:, cols(h)] = v[:, cols(h)] * last_col[...]
        grads = oa[:, cols(h)]
        stepped = nt(grads, state[cols(h), :]) * first_col[...]
        for r in range(tiles):
            here, upto = slice(r * TILE, (r + 1) * TILE), slice(0, (r + 1) * TILE)
            scores = nt(grads[here], v[upto, cols(h)])
            masked = scores.astype(BF16) * same[here, upto]
            adj[here, upto] = masked
            qg[here, cols(h)] = (nn(masked, k[upto, cols(h)]) + stepped[here]).astype(BF16)
        for r in range(tiles):
            here, onward = slice(r * TILE, (r + 1) * TILE), slice(r * TILE, tokens)
            kgl[here, cols(j)] = tn(adj[onward, here], q[onward, cols(h)])
            vgl[here, cols(j)] = tn(weights[h, onward, here], grads[onward])
        normed[:, cols(h)] = (gain[:, cols(h)] * att[:, cols(h)] * inv_col[...]).astype(BF16)
        return carry

    lower = functools.partial(local_backward, base=0, kgl=kgl0, vgl=vgl0)
    upper = functools.partial(local_backward, base=half, kgl=kgl1, vgl=vgl1)
    lax.fori_loop(0, half, lower, 0, unroll=2)
    scan(1)
    lax.fori_loop(0, half, upper, 0, unroll=2)

    def enter_back(head, block):
        back_state[cols(mine + head), :] = block.astype(BF16)

    descend(1, enter_back)
    stat_whole.wait_send()
    for d in reversed(row_offsets):
        head = head_at(d)
        push_down(1, head).wait_recv()
        back_state[cols(other + head), :] = from_sib[1, cols(head), :].astype(BF16)
    settle(1)


def finish(
    normed, qg, kgl0, kgl1, vgl0, vgl1, kl, vl, back_state,
    normed_hbm, qg_hbm, kg_hbm, vg_hbm,
    kg, vg, out_sem,
):
    heads = kg.shape[1] // DH
    stores = [
        pltpu.make_async_copy(normed, normed_hbm, out_sem.at[0]),
        pltpu.make_async_copy(qg, qg_hbm, out_sem.at[1]),
    ]
    for copy in stores:
        copy.start()
    parts = 2
    per_part = heads // parts
    for part, (kgl, vgl) in enumerate(((kgl0, vgl0), (kgl1, vgl1))):
        for j in range(per_part):
            here = slice(j * DH, (j + 1) * DH)
            at = slice((part * per_part + j) * DH, (part * per_part + j + 1) * DH)
            back = back_state[at, :]
            kg[:, at] = (kgl[:, here] + nt(vl[:, at], back)).astype(BF16)
            vg[:, at] = (vgl[:, here] + nn(kl[:, at], back)).astype(BF16)
        done = slice(part * per_part * DH, (part + 1) * per_part * DH)
        for i, (src, dst) in enumerate(((kg, kg_hbm), (vg, vg_hbm))):
            copy = pltpu.make_async_copy(
                src.at[:, done], dst.at[:, done], out_sem.at[2 + 2 * part + i]
            )
            copy.start()
            stores.append(copy)
    for copy in stores:
        copy.wait()


def body(nctx, nhead, query_rows, key_rows, value_rows, out_grad, norm_gain, doc_ids):
    tokens, width = query_rows.shape
    heads = width // DH
    half = heads // 2
    chips = nctx // 2
    rows = half * DH // chips
    blocks = tokens // DH
    grid = (tokens, width)
    half_grid = (tokens, width // 2)
    dma = pltpu.SemaphoreType.DMA
    scratch = [
        *[pltpu.VMEM(grid, BF16)] * 6,
        *[pltpu.VMEM(grid, F32)] * 2,
        pltpu.VMEM((heads, tokens, tokens), BF16),
        pltpu.VMEM((tokens, tokens), BF16),
        pltpu.VMEM((tokens, tokens), BF16),
        pltpu.VMEM((1, width), F32),
        pltpu.VMEM((1, tokens), jnp.int32),
        pltpu.VMEM((half * DH, tokens), BF16),
        *[pltpu.VMEM((tokens, DH), F32)] * 2,
        pltpu.VMEM((tokens, DH), BF16),
        *[pltpu.VMEM((tokens, DH), F32)] * 4,
        pltpu.VMEM((2, heads * DH, DH), F32),
        pltpu.VMEM((2, heads * DH, DH), F32),
        pltpu.VMEM((3 * chips, rows + 8, DH), F32),
        pltpu.VMEM((2, chips, rows + 8, DH), F32),
        *[pltpu.VMEM((2, half * DH, DH), F32)] * 4,
        pltpu.VMEM((heads * DH, DH), BF16),
        *[pltpu.VMEM((8, DH), F32)] * 3,
        pltpu.VMEM((2, 2 * blocks, DH), F32),
        pltpu.VMEM((2 * nhead, 2, 2 * blocks, DH), F32),
        pltpu.VMEM((2, 2 * blocks, DH), F32),
        *[pltpu.VMEM(half_grid, F32)] * 4,
        pltpu.VMEM(half_grid, BF16),
        pltpu.VMEM((half * DH, tokens), BF16),
        pltpu.VMEM((half * DH, DH), BF16),
        *[pltpu.VMEM((tokens, DH), F32)] * 4,
        dma((8,)),
        *[dma((2,))] * 2,
        dma((2, 2)),
        *[dma((2,))] * 3,
        dma((2, half)),
        dma((2,)),
        dma((2, half)),
        dma((2,)),
        *[dma((3,))] * 2,
    ]
    arrays = (
        query_rows, key_rows, value_rows, out_grad,
        norm_gain.reshape(1, width), doc_ids.reshape(1, tokens),
    )
    anywhere = pl.BlockSpec(memory_space=pl.ANY)
    in_hbm = pl.BlockSpec(memory_space=pltpu.HBM)
    in_vmem = pl.BlockSpec(memory_space=pltpu.VMEM)
    parts = pl.pallas_call(
        functools.partial(kernel, nctx, nhead),
        out_shape=[
            *[jax.ShapeDtypeStruct(grid, BF16)] * 2,
            *[jax.ShapeDtypeStruct(half_grid, F32)] * 4,
            *[jax.ShapeDtypeStruct(grid, BF16)] * 2,
            jax.ShapeDtypeStruct((heads * DH, DH), BF16),
        ],
        in_specs=[in_hbm] * 6,
        out_specs=[in_vmem] * 9,
        scratch_shapes=scratch,
        compiler_params=pltpu.CompilerParams(
            collective_id=0, has_side_effects=True, vmem_limit_bytes=44 * 2**20
        ),
        name="attend",
    )(*[pltpu.with_memory_space_constraint(array, pltpu.HBM) for array in arrays])
    return pl.pallas_call(
        finish,
        out_shape=[jax.ShapeDtypeStruct(grid, BF16)] * 4,
        in_specs=[in_vmem] * 9,
        out_specs=[anywhere] * 4,
        scratch_shapes=[*[pltpu.VMEM(grid, BF16)] * 2, dma((6,))],
        compiler_params=pltpu.CompilerParams(vmem_limit_bytes=16 * 2**20),
        name="finish",
    )(*parts)


def solution(mesh):
    nctx, nhead = mesh.shape["ctx"], mesh.shape["head"]
    placed = (
        P("ctx", "head"),
        P("ctx", "head"),
        P("ctx", "head"),
        P("ctx", "head"),
        P("head"),
        P("ctx"),
    )
    return jax.shard_map(
        functools.partial(body, nctx, nhead),
        mesh=mesh,
        in_specs=placed,
        out_specs=(P("ctx", "head"), P("ctx", "head"), P("ctx", "head"), P("ctx", "head")),
        check_vma=False,
    )
```

```python
import functools
import math

import jax
import jax.numpy as jnp
from jax import lax
from jax.experimental import pallas as pl
from jax.experimental.pallas import tpu as pltpu
from jax.sharding import PartitionSpec as P

DH = 128
TILE = 256
epsilon = 1e-05
MESH = pl.DeviceIdType.MESH
F32 = jnp.float32
BF16 = jnp.bfloat16


def nn(a, b):
    return lax.dot_general(a, b, (((1,), (0,)), ((), ())), preferred_element_type=F32)


def nt(a, b):
    return lax.dot_general(a, b, (((1,), (1,)), ((), ())), preferred_element_type=F32)


def tn(a, b):
    return lax.dot_general(a, b, (((0,), (0,)), ((), ())), preferred_element_type=F32)


def equal(a, b):
    return jnp.where(a == b, 1.0, 0.0).astype(F32)


def row_sums(values):
    ones = jnp.ones((8, DH), BF16)
    high = values.astype(BF16)
    low = (values - high.astype(F32)).astype(BF16)
    return (nt(ones, high) + nt(ones, low))[0:1, :]


def far_first(chips):
    across = math.isqrt(chips)
    along = chips // across

    def hops(offset):
        dy, dx = offset
        return min(dy, along - dy) + min(dx, across - dx)

    offsets = [(dy, dx) for dy in range(along) for dx in range(across) if dy + dx > 0]
    return sorted(offsets, key=hops, reverse=True)


def kernel(
    nctx, nhead,
    q_hbm, k_hbm, v_hbm, dy_hbm, gain_hbm, docs_hbm,
    normed, qg, kgl0, kgl1, vgl0, vgl1, kl, vl, back_state,
    q, k, v, dy, qf, oa, att, scaled, weights, adj, same, gain, docs, qf_turned, dcol,
    first_col, last_col, inv_col, adj_col, sq_acc, gr_acc,
    piece, sib_piece, total, slices, scanned, landed, to_sib, from_sib, state,
    my_info, sib_info, chip_info, stat_out, stat_in, stat_sum,
    qf_wide, qf_in, att_sib, scaled_sib, qf_sib, turned_sib,
    sq_sib, gr_sib, inv_sib, adj_sib,
    in_sem, sib_sem, up_send, up_recv, a_send, a_recv, b_send, b_recv,
    down_send, down_recv, stat_sem, swap_send, swap_recv,
):
    tokens, width = q.shape
    heads = width // DH
    half = heads // 2
    chips = nctx // 2
    across = math.isqrt(chips)
    along = chips // across
    rows = half * DH // chips
    blocks = tokens // DH
    tiles = tokens // TILE
    me = lax.axis_index("ctx")
    z = lax.axis_index("head")
    chip = lax.div(me, 2)
    core = lax.rem(me, 2)
    sibling = me + 1 - 2 * core
    mine, other = core * half, (1 - core) * half
    here_y, here_x = lax.div(chip, across), lax.rem(chip, across)
    row_offsets = sorted(range(along), key=lambda d: -min(d, along - d))
    groups = [row_offsets[:1], row_offsets[1:-1], row_offsets[-1:]]
    column_offsets = sorted(range(across), key=lambda d: -min(d, across - d))

    def cols(h):
        return pl.ds(pl.multiple_of(h * DH, DH), DH)

    def side(s):
        return pl.ds(pl.multiple_of(s * (width // 2), width // 2), width // 2)

    def slot(i):
        return pl.ds(pl.multiple_of(i * rows, rows), rows)

    def chip_at(offset):
        y = lax.rem(here_y + offset[0], along)
        x = lax.rem(here_x + offset[1], across)
        return y * across + x

    def head_at(d):
        return lax.rem(here_y + d, along)

    def to_chip(i):
        return {"ctx": 2 * i + core}

    chip_offsets = far_first(chips)
    head_offsets = sorted(range(1, nhead), key=lambda d: -min(d, nhead - d))

    def load(i, src, dst, s):
        return pltpu.make_async_copy(src.at[:, side(s)], dst.at[:, side(s)], in_sem.at[i])

    first_loads = [load(0, k_hbm, k, 1 - core), load(1, v_hbm, v, 1 - core)]
    docs_load = pltpu.make_async_copy(docs_hbm, docs, in_sem.at[2])
    own_loads = [load(3, k_hbm, k, core), load(4, v_hbm, v, core)]
    later_loads = [
        pltpu.make_async_copy(q_hbm, q, in_sem.at[5]),
        pltpu.make_async_copy(dy_hbm, dy, in_sem.at[6]),
        pltpu.make_async_copy(gain_hbm, gain, in_sem.at[7]),
    ]
    docs_load.start()
    for copy in first_loads + own_loads:
        copy.start()

    barrier = pltpu.get_barrier_semaphore()

    def greet(device):
        pl.semaphore_signal(barrier, inc=1, device_id=device, device_id_type=MESH)

    for offset in chip_offsets:
        greet({"ctx": 2 * chip_at(offset)})
    for offset in head_offsets:
        greet({"ctx": 2 * chip, "head": lax.rem(z + offset, nhead)})
    greet({"ctx": sibling})
    for copy in later_loads:
        copy.start()

    docs_load.wait()
    drow = docs[...].astype(F32)
    first_id = drow[:, 0:1]
    last_id = drow[:, tokens - 1 : tokens]
    my_info[0:1, :] = jnp.broadcast_to(first_id, (1, DH))
    my_info[1:2, :] = jnp.broadcast_to(last_id, (1, DH))
    for b in range(blocks):
        block = slice(b * DH, (b + 1) * DH)
        dcol[block, :] = jnp.broadcast_to(drow[:, block], (DH, DH)).T
    first_col[...] = equal(dcol[...], first_id)
    last_col[...] = equal(dcol[...], last_id).astype(BF16)

    def to_sibling(src, dst, send_sem, recv_sem):
        return pltpu.make_async_remote_copy(
            src_ref=src,
            dst_ref=dst,
            send_sem=send_sem,
            recv_sem=recv_sem,
            device_id={"ctx": sibling},
            device_id_type=MESH,
        )

    def up_heads(turn, g, first, last):
        at = slice(first * DH, last * DH)
        return to_sibling(
            piece.at[turn, at, :], sib_piece.at[turn, at, :],
            up_send.at[turn], up_recv.at[turn, g],
        )

    def push_down(turn, head):
        return to_sibling(
            to_sib.at[turn, cols(head), :], from_sib.at[turn, cols(head), :],
            down_send.at[turn], down_recv.at[turn, head],
        )

    def send_slice(src, dst, send_sem, recv_sem, device):
        pltpu.make_async_remote_copy(
            src_ref=src,
            dst_ref=dst,
            send_sem=send_sem,
            recv_sem=recv_sem,
            device_id=device,
            device_id_type=MESH,
        ).start()

    def sent_rows(turn):
        return slice(0, rows + 8) if turn == 0 else slice(0, rows)

    def slices_whole(turn, count):
        part = (slice(0, count), sent_rows(turn))
        return to_sibling(total.at[part], total.at[part], a_send.at[turn], a_recv.at[turn])

    def back_whole(turn, count, row):
        part = (turn, slice(0, count * rows))
        return to_sibling(
            scanned.at[part], landed.at[part], b_send.at[turn], b_recv.at[turn, row]
        )

    def swap(n):
        src, dst = (
            (scaled.at[:, side(1 - core)], scaled_sib),
            (qf_wide, qf_in),
            (att.at[:, side(1 - core)], att_sib),
        )[n]
        return to_sibling(src, dst, swap_send.at[n], swap_recv.at[n])

    def orders(turn):
        return (0, 1, 2, 3) if turn == 0 else (3, 2, 1, 0)

    def is_near(turn):
        return jnp.full((1, DH), core if turn == 0 else 1 - core, jnp.int32) == 0

    def ids_of(row):
        return chip_info[row : row + 1, :]

    def add_up(turn, head, place):
        _, near_last, _, far_last = orders(turn)
        joined = equal(ids_of(near_last), ids_of(far_last))
        own_share = jnp.where(is_near(turn), joined, 1.0)
        sib_share = jnp.where(is_near(turn), 1.0, joined)
        for x in range(across):
            part = pl.ds(pl.multiple_of(head * DH + x * rows, rows), rows)
            total[place + x, 0:rows, :] = (
                piece[turn, part, :] * own_share + sib_piece[turn, part, :] * sib_share
            )

    def ascend_forward():
        for copy in first_loads:
            copy.wait()

        @pl.when(core == 1)
        def _():
            for h in range(half):
                make_piece(h)
            pl.semaphore_wait(barrier, 1)
            sib_ids.start()
            up_heads(0, 0, 0, half).start()
            for copy in own_loads:
                copy.wait()
            for h in range(half, heads):
                make_piece(h)
            up_heads(0, 1, half, heads).start()

        @pl.when(core == 0)
        def _():
            for copy in own_loads:
                copy.wait()
            for h in range(heads):
                make_piece(h)
            sib_ids.wait_recv()
            chip_info[0:2, :] = my_info[0:2, :]
            chip_info[2:4, :] = sib_info[0:2, :]
            up_heads(0, 0, 0, half).wait_recv()
            for head in range(half):
                add_up(0, head, head * across)
            up_heads(0, 1, half, heads).wait_recv()
            for head in range(half, heads):
                add_up(0, head, head * across)
            for i in range(2 * chips):
                total[i, rows : rows + 8, :] = chip_info[...]
            pl.semaphore_wait(barrier, 1 + 2 * (chips - 1) + 2 * (nhead - 1))
            for offset in chip_offsets:
                i = chip_at(offset)
                for a in range(2):
                    send_slice(
                        total.at[a * chips + i], slices.at[0, chip],
                        a_send.at[0], a_recv.at[0], {"ctx": 2 * i + a},
                    )
            send_slice(
                total.at[chips + chip], slices.at[0, chip],
                a_send.at[0], a_recv.at[0], {"ctx": sibling},
            )
            up_heads(0, 0, half, heads).start()
            slices[0, chip] = total[chip]

    def ascend_backward(make):
        for group in groups:
            for d in group:
                make(head_at(d))
            for d in group:
                add_up(1, mine + head_at(d), 2 * chips + head_at(d) * across)
            for offset in chip_offsets:
                if offset[0] in group:
                    i = chip_at(offset)
                    send_slice(
                        total.at[2 * chips + i, sent_rows(1)], slices.at[1, chip, sent_rows(1)],
                        a_send.at[1], a_recv.at[1], to_chip(i),
                    )
        slices[1, chip] = total[2 * chips + chip]

    def scan(turn):
        near_first, _, _, far_last = orders(turn)
        if turn == 0:

            @pl.when(core == 0)
            def _():
                slices_whole(0, chips - 1).wait_recv()

            @pl.when(core == 1)
            def _():
                slices_whole(0, chips).wait_recv()
                up_heads(0, 0, half, heads).wait_recv()
                chip_info[...] = slices[0, chip, rows : rows + 8, :]

        else:
            slices_whole(1, chips - 1).wait_recv()
        running = jnp.zeros((rows, DH), F32)
        before = jnp.full((1, DH), -1.0, F32)
        for j in range(chips):
            i = j if turn == 0 else chips - 1 - j
            ids = slices[0, i, rows : rows + 8, :]
            enters = ids[near_first : near_first + 1, :]
            leaves = ids[far_last : far_last + 1, :]
            here = slice(i * rows, (i + 1) * rows)
            scanned[turn, here, :] = running * equal(before, enters)
            running = slices[turn, i, 0:rows, :] + running * equal(before, leaves)
            before = leaves
        for offset in chip_offsets:
            i = chip_at(offset)
            send_slice(
                scanned.at[turn, slot(i), :], landed.at[turn, slot(chip), :],
                b_send.at[turn], b_recv.at[turn, here_y], to_chip(i),
            )
        landed[turn, slot(chip), :] = scanned[turn, slot(chip), :]

    def descend(turn, into, then):
        near_first, near_last, far_first, _ = orders(turn)
        next_to = equal(ids_of(near_last), ids_of(far_first))
        through = equal(ids_of(near_first), ids_of(far_first))
        near = is_near(turn)
        own_enter = jnp.where(near, 1.0, through)
        own_sib = jnp.where(near, 0.0, next_to)
        sib_enter = jnp.where(near, through, 1.0)
        sib_own = jnp.where(near, next_to, 0.0)
        for group in reversed(groups):
            for d in group:
                head = head_at(d)
                at = cols(head)
                back_whole(turn, across - (d == 0), head).wait_recv()
                to_sib[turn, at, :] = (
                    landed[turn, at, :] * sib_enter + piece[turn, cols(mine + head), :] * sib_own
                )
                push_down(turn, head).start()
                beyond = sib_piece[turn, cols(mine + head), :]
                into(head, landed[turn, at, :] * own_enter + beyond * own_sib)
            for d in group:
                then(head_at(d))

    sib_ids = to_sibling(my_info, sib_info, sib_sem.at[0], sib_sem.at[1])

    def settle(turn):
        whole = to_sibling(
            to_sib.at[turn], from_sib.at[turn], down_send.at[turn], down_recv.at[turn, 0]
        )
        whole.wait_send()
        back_whole(turn, chips - 1, 0).wait_send()
        if turn == 0:

            @pl.when(core == 0)
            def _():
                up_heads(0, 0, half, heads).wait_send()
                slices_whole(0, 2 * chips - 1).wait_send()

            @pl.when(core == 1)
            def _():
                up_heads(0, 0, 0, heads).wait_send()
                sib_ids.wait_send()

            for n in range(3):
                swap(n).wait_send()
        else:
            slices_whole(1, chips - 1).wait_send()

    def make_piece(h):
        piece[0, cols(h), :] = tn(k[:, cols(h)] * last_col[...], v[:, cols(h)])

    ascend_forward()

    later = lax.broadcasted_iota(jnp.int32, (tokens, DH), 0)
    for b in range(blocks):
        block = slice(b * DH, (b + 1) * DH)
        earlier = lax.broadcasted_iota(jnp.int32, (tokens, DH), 1) + b * DH
        ids = jnp.broadcast_to(drow[:, block], (tokens, DH))
        same[:, block] = jnp.where((dcol[...] == ids) & (later >= earlier), 1.0, 0.0).astype(BF16)
    for copy in later_loads:
        copy.wait()

    def prepare(j, carry, base):
        h = base + j
        qf[:, cols(h)] = q[:, cols(h)] * first_col[...].astype(BF16)
        scaled[:, cols(h)] = gain[:, cols(h)] * dy[:, cols(h)].astype(F32)
        return carry

    def widen(j, carry):
        qf_wide[:, cols(j)] = qf[:, cols(other + j)].astype(F32)
        return carry

    lax.fori_loop(0, half, functools.partial(prepare, base=other), 0)
    lax.fori_loop(0, half, widen, 0)
    swap(0).start()
    swap(1).start()

    def local_forward(j, carry, base):
        h = base + j
        for r in range(tiles):
            here, upto = slice(r * TILE, (r + 1) * TILE), slice(0, (r + 1) * TILE)
            scores = nt(q[here, cols(h)], k[upto, cols(h)])
            masked = scores.astype(BF16) * same[here, upto]
            weights[h, here, upto] = masked
            att[here, cols(h)] = nn(masked, v[upto, cols(h)])
        return carry

    lax.fori_loop(0, half, functools.partial(local_forward, base=other), 0, unroll=2)
    swap(2).start()
    scan(0)
    lax.fori_loop(0, half, functools.partial(prepare, base=mine), 0)
    lax.fori_loop(0, half, functools.partial(local_forward, base=mine), 0, unroll=2)
    for n in range(3):
        swap(n).wait_recv()

    def turn_queries(j, carry):
        queries = qf_in[:, cols(j)].astype(BF16)
        qf_sib[:, cols(j)] = queries
        turned_sib[cols(j), :] = queries.T
        qf_turned[cols(j), :] = qf[:, cols(mine + j)].T
        return carry

    lax.fori_loop(0, half, turn_queries, 0)

    def enter(head, block):
        state[cols(mine + head), :] = block.astype(BF16)

    def attend(head):
        h = mine + head
        whole = att[:, cols(h)] + nn(qf[:, cols(h)], state[cols(h), :])
        att[:, cols(h)] = whole
        sq_acc[...] += whole * whole
        gr_acc[...] += scaled[:, cols(h)] * whole
        entering = to_sib[0, cols(head), :].astype(BF16)
        whole = att_sib[:, cols(head)] + nn(qf_sib[:, cols(head)], entering)
        att_sib[:, cols(head)] = whole
        sq_sib[...] += whole * whole
        gr_sib[...] += scaled_sib[:, cols(head)] * whole

    sq_acc[...] = jnp.zeros_like(sq_acc)
    gr_acc[...] = jnp.zeros_like(gr_acc)
    sq_sib[...] = jnp.zeros_like(sq_sib)
    gr_sib[...] = jnp.zeros_like(gr_sib)
    descend(0, enter, attend)
    for at, squares, grads in ((core, sq_acc, gr_acc), (1 - core, sq_sib, gr_sib)):
        square_sums, grad_sums = row_sums(squares[...]), row_sums(grads[...])
        for b in range(blocks):
            block = slice(b * DH, (b + 1) * DH)
            stat_out[at, b : b + 1, :] = square_sums[:, block]
            stat_out[at, blocks + b : blocks + b + 1, :] = grad_sums[:, block]

    def send_stat(device):
        pltpu.make_async_remote_copy(
            src_ref=stat_out,
            dst_ref=stat_in.at[2 * z + core],
            send_sem=stat_sem.at[0],
            recv_sem=stat_sem.at[1],
            device_id=device,
            device_id_type=MESH,
        ).start()

    for offset in head_offsets:
        for a in (core, 1 - core):
            send_stat({"ctx": 2 * chip + a, "head": lax.rem(z + offset, nhead)})
    send_stat({"ctx": sibling})
    stat_in[2 * z + core] = stat_out[...]
    settle(0)
    for d in reversed(row_offsets):
        head = head_at(d)
        push_down(0, head).wait_recv()
        state[cols(other + head), :] = from_sib[0, cols(head), :].astype(BF16)
    for j in range(half):
        att[:, cols(other + j)] += nn(qf[:, cols(other + j)], state[cols(other + j), :])
    stat_whole = to_sibling(
        stat_in.at[0 : 2 * nhead - 1], stat_in.at[0 : 2 * nhead - 1],
        stat_sem.at[0], stat_sem.at[1],
    )
    stat_whole.wait_recv()
    sums = stat_in[0]
    for at in range(1, 2 * nhead):
        sums = sums + stat_in[at]
    stat_sum[...] = sums / (width * nhead)
    for at, inv_to, adj_to in ((core, inv_col, adj_col), (1 - core, inv_sib, adj_sib)):
        means = stat_sum[at]
        inv = lax.rsqrt(means[0:blocks, :] + epsilon)
        factor = inv * inv * inv * means[blocks : 2 * blocks, :]
        turned = jnp.concatenate([inv, factor] * (DH // (2 * blocks)), axis=0).T
        for b in range(blocks):
            block = slice(b * DH, (b + 1) * DH)
            inv_to[block, :] = jnp.broadcast_to(turned[:, b : b + 1], (DH, DH))
            adj_to[block, :] = jnp.broadcast_to(
                turned[:, blocks + b : blocks + b + 1], (DH, DH)
            )

    def adjoint(h):
        return (inv_col[...] * scaled[:, cols(h)] - att[:, cols(h)] * adj_col[...]).astype(BF16)

    def back_pieces(head):
        grads = adjoint(mine + head)
        oa[:, cols(mine + head)] = grads
        piece[1, cols(mine + head), :] = nn(qf_turned[cols(head), :], grads)
        grads = (
            inv_sib[...] * scaled_sib[:, cols(head)] - att_sib[:, cols(head)] * adj_sib[...]
        ).astype(BF16)
        sib_piece[1, cols(mine + head), :] = nn(turned_sib[cols(head), :], grads)

    ascend_backward(back_pieces)
    for j in range(half):
        oa[:, cols(other + j)] = adjoint(other + j)

    def local_backward(j, carry, base, kgl, vgl):
        h = base + j
        kl[:, cols(h)] = k[:, cols(h)] * last_col[...]
        vl[:, cols(h)] = v[:, cols(h)] * last_col[...]
        grads = oa[:, cols(h)]
        stepped = nt(grads, state[cols(h), :]) * first_col[...]
        for r in range(tiles):
            here, upto = slice(r * TILE, (r + 1) * TILE), slice(0, (r + 1) * TILE)
            scores = nt(grads[here], v[upto, cols(h)])
            masked = scores.astype(BF16) * same[here, upto]
            adj[here, upto] = masked
            qg[here, cols(h)] = (nn(masked, k[upto, cols(h)]) + stepped[here]).astype(BF16)
        for r in range(tiles):
            here, onward = slice(r * TILE, (r + 1) * TILE), slice(r * TILE, tokens)
            kgl[here, cols(j)] = tn(adj[onward, here], q[onward, cols(h)])
            vgl[here, cols(j)] = tn(weights[h, onward, here], grads[onward])
        normed[:, cols(h)] = (gain[:, cols(h)] * att[:, cols(h)] * inv_col[...]).astype(BF16)
        return carry

    lower = functools.partial(local_backward, base=0, kgl=kgl0, vgl=vgl0)
    upper = functools.partial(local_backward, base=half, kgl=kgl1, vgl=vgl1)
    lax.fori_loop(0, half, lower, 0, unroll=2)
    scan(1)
    lax.fori_loop(0, half, upper, 0, unroll=2)

    def enter_back(head, block):
        back_state[cols(mine + head), :] = block.astype(BF16)

    descend(1, enter_back, lambda head: None)
    stat_whole.wait_send()
    for d in reversed(row_offsets):
        head = head_at(d)
        push_down(1, head).wait_recv()
        back_state[cols(other + head), :] = from_sib[1, cols(head), :].astype(BF16)
    settle(1)


def finish(
    normed, qg, kgl0, kgl1, vgl0, vgl1, kl, vl, back_state,
    normed_hbm, qg_hbm, kg_hbm, vg_hbm,
    kg, vg, out_sem,
):
    heads = kg.shape[1] // DH
    stores = [
        pltpu.make_async_copy(normed, normed_hbm, out_sem.at[0]),
        pltpu.make_async_copy(qg, qg_hbm, out_sem.at[1]),
    ]
    for copy in stores:
        copy.start()
    parts = 2
    per_part = heads // parts
    for part, (kgl, vgl) in enumerate(((kgl0, vgl0), (kgl1, vgl1))):
        for j in range(per_part):
            here = slice(j * DH, (j + 1) * DH)
            at = slice((part * per_part + j) * DH, (part * per_part + j + 1) * DH)
            back = back_state[at, :]
            kg[:, at] = (kgl[:, here] + nt(vl[:, at], back)).astype(BF16)
            vg[:, at] = (vgl[:, here] + nn(kl[:, at], back)).astype(BF16)
        done = slice(part * per_part * DH, (part + 1) * per_part * DH)
        for i, (src, dst) in enumerate(((kg, kg_hbm), (vg, vg_hbm))):
            copy = pltpu.make_async_copy(
                src.at[:, done], dst.at[:, done], out_sem.at[2 + 2 * part + i]
            )
            copy.start()
            stores.append(copy)
    for copy in stores:
        copy.wait()


def body(nctx, nhead, query_rows, key_rows, value_rows, out_grad, norm_gain, doc_ids):
    tokens, width = query_rows.shape
    heads = width // DH
    half = heads // 2
    chips = nctx // 2
    rows = half * DH // chips
    blocks = tokens // DH
    grid = (tokens, width)
    half_grid = (tokens, width // 2)
    dma = pltpu.SemaphoreType.DMA
    scratch = [
        *[pltpu.VMEM(grid, BF16)] * 6,
        *[pltpu.VMEM(grid, F32)] * 2,
        pltpu.VMEM((heads, tokens, tokens), BF16),
        pltpu.VMEM((tokens, tokens), BF16),
        pltpu.VMEM((tokens, tokens), BF16),
        pltpu.VMEM((1, width), F32),
        pltpu.VMEM((1, tokens), jnp.int32),
        pltpu.VMEM((half * DH, tokens), BF16),
        *[pltpu.VMEM((tokens, DH), F32)] * 2,
        pltpu.VMEM((tokens, DH), BF16),
        *[pltpu.VMEM((tokens, DH), F32)] * 4,
        pltpu.VMEM((2, heads * DH, DH), F32),
        pltpu.VMEM((2, heads * DH, DH), F32),
        pltpu.VMEM((3 * chips, rows + 8, DH), F32),
        pltpu.VMEM((2, chips, rows + 8, DH), F32),
        *[pltpu.VMEM((2, half * DH, DH), F32)] * 4,
        pltpu.VMEM((heads * DH, DH), BF16),
        *[pltpu.VMEM((8, DH), F32)] * 3,
        pltpu.VMEM((2, 2 * blocks, DH), F32),
        pltpu.VMEM((2 * nhead, 2, 2 * blocks, DH), F32),
        pltpu.VMEM((2, 2 * blocks, DH), F32),
        *[pltpu.VMEM(half_grid, F32)] * 4,
        pltpu.VMEM(half_grid, BF16),
        pltpu.VMEM((half * DH, tokens), BF16),
        *[pltpu.VMEM((tokens, DH), F32)] * 4,
        dma((8,)),
        *[dma((2,))] * 2,
        dma((2, 2)),
        *[dma((2,))] * 3,
        dma((2, half)),
        dma((2,)),
        dma((2, half)),
        dma((2,)),
        *[dma((3,))] * 2,
    ]
    arrays = (
        query_rows, key_rows, value_rows, out_grad,
        norm_gain.reshape(1, width), doc_ids.reshape(1, tokens),
    )
    anywhere = pl.BlockSpec(memory_space=pl.ANY)
    in_hbm = pl.BlockSpec(memory_space=pltpu.HBM)
    in_vmem = pl.BlockSpec(memory_space=pltpu.VMEM)
    parts = pl.pallas_call(
        functools.partial(kernel, nctx, nhead),
        out_shape=[
            *[jax.ShapeDtypeStruct(grid, BF16)] * 2,
            *[jax.ShapeDtypeStruct(half_grid, F32)] * 4,
            *[jax.ShapeDtypeStruct(grid, BF16)] * 2,
            jax.ShapeDtypeStruct((heads * DH, DH), BF16),
        ],
        in_specs=[in_hbm] * 6,
        out_specs=[in_vmem] * 9,
        scratch_shapes=scratch,
        compiler_params=pltpu.CompilerParams(
            collective_id=0, has_side_effects=True, vmem_limit_bytes=44 * 2**20
        ),
        name="attend",
    )(*[pltpu.with_memory_space_constraint(array, pltpu.HBM) for array in arrays])
    return pl.pallas_call(
        finish,
        out_shape=[jax.ShapeDtypeStruct(grid, BF16)] * 4,
        in_specs=[in_vmem] * 9,
        out_specs=[anywhere] * 4,
        scratch_shapes=[*[pltpu.VMEM(grid, BF16)] * 2, dma((6,))],
        compiler_params=pltpu.CompilerParams(vmem_limit_bytes=16 * 2**20),
        name="finish",
    )(*parts)


def solution(mesh):
    nctx, nhead = mesh.shape["ctx"], mesh.shape["head"]
    placed = (
        P("ctx", "head"),
        P("ctx", "head"),
        P("ctx", "head"),
        P("ctx", "head"),
        P("head"),
        P("ctx"),
    )
    return jax.shard_map(
        functools.partial(body, nctx, nhead),
        mesh=mesh,
        in_specs=placed,
        out_specs=(P("ctx", "head"), P("ctx", "head"), P("ctx", "head"), P("ctx", "head")),
        check_vma=False,
    )
```

```python
import functools
import math

import jax
import jax.numpy as jnp
from jax import lax
from jax.experimental import pallas as pl
from jax.experimental.pallas import tpu as pltpu
from jax.sharding import PartitionSpec as P

DH = 128
TILE = 256
epsilon = 1e-05
MESH = pl.DeviceIdType.MESH
F32 = jnp.float32
BF16 = jnp.bfloat16


def nn(a, b):
    return lax.dot_general(a, b, (((1,), (0,)), ((), ())), preferred_element_type=F32)


def nt(a, b):
    return lax.dot_general(a, b, (((1,), (1,)), ((), ())), preferred_element_type=F32)


def tn(a, b):
    return lax.dot_general(a, b, (((0,), (0,)), ((), ())), preferred_element_type=F32)


def equal(a, b):
    return jnp.where(a == b, 1.0, 0.0).astype(F32)


def row_sums(values):
    ones = jnp.ones((8, DH), BF16)
    high = values.astype(BF16)
    low = (values - high.astype(F32)).astype(BF16)
    return (nt(ones, high) + nt(ones, low))[0:1, :]


def far_first(chips):
    across = math.isqrt(chips)
    along = chips // across

    def hops(offset):
        dy, dx = offset
        return min(dy, along - dy) + min(dx, across - dx)

    offsets = [(dy, dx) for dy in range(along) for dx in range(across) if dy + dx > 0]
    ordered = []
    for dy, dx in sorted(offsets, key=hops, reverse=True):
        for offset in ((dy, dx), (-dy % along, -dx % across)):
            if offset not in ordered:
                ordered.append(offset)
    return ordered


def kernel(
    nctx, nhead,
    q_hbm, k_hbm, v_hbm, dy_hbm, gain_hbm, docs_hbm,
    normed, qg, kgl0, kgl1, vgl0, vgl1, kl, vl, back_state,
    q, k, v, dy, qf, oa, att, scaled, weights, adj, same, gain, docs, qf_turned, dcol,
    first_col, last_col, inv_col, adj_col, sq_acc, gr_acc,
    piece, sib_piece, total, slices, scanned, landed, to_sib, from_sib, state,
    my_info, sib_info, chip_info, stat_out, stat_in, stat_sum,
    qf_wide, qf_in, att_sib, scaled_sib, qf_sib, turned_sib,
    sq_sib, gr_sib, inv_sib, adj_sib,
    in_sem, sib_sem, up_sem, go_sem, a_send, a_recv, b_send, b_recv,
    down_send, down_recv, stat_sem, swap_send, swap_recv,
):
    tokens, width = q.shape
    heads = width // DH
    half = heads // 2
    chips = nctx // 2
    across = math.isqrt(chips)
    along = chips // across
    rows = half * DH // chips
    blocks = tokens // DH
    tiles = tokens // TILE
    me = lax.axis_index("ctx")
    z = lax.axis_index("head")
    chip = lax.div(me, 2)
    core = lax.rem(me, 2)
    sibling = me + 1 - 2 * core
    mine, other = core * half, (1 - core) * half
    here_y, here_x = lax.div(chip, across), lax.rem(chip, across)
    row_offsets = sorted(range(along), key=lambda d: -min(d, along - d))
    groups = [row_offsets[:1], row_offsets[1:-1], row_offsets[-1:]]
    column_offsets = sorted(range(across), key=lambda d: -min(d, across - d))

    def cols(h):
        return pl.ds(pl.multiple_of(h * DH, DH), DH)

    def side(s):
        return pl.ds(pl.multiple_of(s * (width // 2), width // 2), width // 2)

    def slot(i):
        return pl.ds(pl.multiple_of(i * rows, rows), rows)

    def chip_at(offset):
        y = lax.rem(here_y + offset[0], along)
        x = lax.rem(here_x + offset[1], across)
        return y * across + x

    def head_at(d):
        return lax.rem(here_y + d, along)

    def to_chip(i):
        return {"ctx": 2 * i + core}

    chip_offsets = far_first(chips)
    head_offsets = sorted(range(1, nhead), key=lambda d: -min(d, nhead - d))

    def load(i, src, dst, s):
        return pltpu.make_async_copy(src.at[:, side(s)], dst.at[:, side(s)], in_sem.at[i])

    first_loads = [load(0, k_hbm, k, 1 - core), load(1, v_hbm, v, 1 - core)]
    docs_load = pltpu.make_async_copy(docs_hbm, docs, in_sem.at[2])
    own_loads = [load(3, k_hbm, k, core), load(4, v_hbm, v, core)]
    later_loads = [
        pltpu.make_async_copy(q_hbm, q, in_sem.at[5]),
        pltpu.make_async_copy(dy_hbm, dy, in_sem.at[6]),
        pltpu.make_async_copy(gain_hbm, gain, in_sem.at[7]),
    ]
    docs_load.start()
    for copy in first_loads + own_loads:
        copy.start()

    barrier = pltpu.get_barrier_semaphore()

    def greet(device):
        pl.semaphore_signal(barrier, inc=1, device_id=device, device_id_type=MESH)

    for offset in chip_offsets:
        greet({"ctx": 2 * chip_at(offset)})
    for offset in head_offsets:
        greet({"ctx": 2 * chip, "head": lax.rem(z + offset, nhead)})
    greet({"ctx": sibling})
    for copy in later_loads:
        copy.start()

    docs_load.wait()
    drow = docs[...].astype(F32)
    first_id = drow[:, 0:1]
    last_id = drow[:, tokens - 1 : tokens]
    my_info[0:1, :] = jnp.broadcast_to(first_id, (1, DH))
    my_info[1:2, :] = jnp.broadcast_to(last_id, (1, DH))
    for b in range(blocks):
        block = slice(b * DH, (b + 1) * DH)
        dcol[block, :] = jnp.broadcast_to(drow[:, block], (DH, DH)).T
    first_col[...] = equal(dcol[...], first_id)
    last_col[...] = equal(dcol[...], last_id).astype(BF16)

    def to_sibling(src, dst, send_sem, recv_sem):
        return pltpu.make_async_remote_copy(
            src_ref=src,
            dst_ref=dst,
            send_sem=send_sem,
            recv_sem=recv_sem,
            device_id={"ctx": sibling},
            device_id_type=MESH,
        )

    def up_half():
        at = pl.ds(pl.multiple_of(other * DH, half * DH), half * DH)
        return to_sibling(piece.at[0, at, :], sib_piece.at[0, at, :], up_sem.at[0], up_sem.at[1])

    def push_down(turn, head):
        return to_sibling(
            to_sib.at[turn, cols(head), :], from_sib.at[turn, cols(head), :],
            down_send.at[turn], down_recv.at[turn, head],
        )

    def send_slice(src, dst, send_sem, recv_sem, device):
        pltpu.make_async_remote_copy(
            src_ref=src,
            dst_ref=dst,
            send_sem=send_sem,
            recv_sem=recv_sem,
            device_id=device,
            device_id_type=MESH,
        ).start()

    def sent_rows(turn):
        return slice(0, rows + 8) if turn == 0 else slice(0, rows)

    def slices_whole(turn, count):
        part = (slice(0, count), sent_rows(turn))
        return to_sibling(total.at[part], total.at[part], a_send.at[turn], a_recv.at[turn])

    def back_whole(turn, count, row):
        part = (turn, slice(0, count * rows))
        return to_sibling(
            scanned.at[part], landed.at[part], b_send.at[turn], b_recv.at[turn, row]
        )

    def swap(n):
        src, dst = (
            (scaled.at[:, side(1 - core)], scaled_sib),
            (qf_wide, qf_in),
            (att.at[:, side(1 - core)], att_sib),
        )[n]
        return to_sibling(src, dst, swap_send.at[n], swap_recv.at[n])

    def orders(turn):
        return (0, 1, 2, 3) if turn == 0 else (3, 2, 1, 0)

    def is_near(turn):
        return jnp.full((1, DH), core if turn == 0 else 1 - core, jnp.int32) == 0

    def ids_of(row):
        return chip_info[row : row + 1, :]

    def add_up(turn, head, place):
        _, near_last, _, far_last = orders(turn)
        joined = equal(ids_of(near_last), ids_of(far_last))
        own_share = jnp.where(is_near(turn), joined, 1.0)
        sib_share = jnp.where(is_near(turn), 1.0, joined)
        for x in range(across):
            part = pl.ds(pl.multiple_of(head * DH + x * rows, rows), rows)
            total[place + x, 0:rows, :] = (
                piece[turn, part, :] * own_share + sib_piece[turn, part, :] * sib_share
            )

    def ascend_forward():
        for copy in first_loads:
            copy.wait()
        for j in range(half):
            make_piece(other + j)

        @pl.when(core == 1)
        def _():
            pl.semaphore_wait(barrier, 1)
            sib_ids.start()
            up_half().start()

        for copy in own_loads:
            copy.wait()

        @pl.when(core == 0)
        def _():
            sib_ids.wait_recv()
            sib_ids.start()
            up_half().start()

        for j in range(half):
            make_piece(mine + j)

        @pl.when(core == 1)
        def _():
            sib_ids.wait_recv()

        near = is_near(0)
        for at in range(2):
            here, there = my_info[at : at + 1, :], sib_info[at : at + 1, :]
            chip_info[at : at + 1, :] = jnp.where(near, here, there)
            chip_info[at + 2 : at + 3, :] = jnp.where(near, there, here)
        for i in range(chips):
            total[i, rows : rows + 8, :] = chip_info[...]
        up_half().wait_recv()
        for head in range(half):
            add_up(0, mine + head, head * across)

        @pl.when(core == 0)
        def _():
            pl.semaphore_wait(barrier, 1 + 2 * (chips - 1) + 2 * (nhead - 1))
            pl.semaphore_signal(go_sem, inc=1, device_id={"ctx": sibling}, device_id_type=MESH)

        @pl.when(core == 1)
        def _():
            pl.semaphore_wait(go_sem, 1)

        for offset in chip_offsets:
            i = chip_at(offset)
            send_slice(
                total.at[i], slices.at[0, chip], a_send.at[0], a_recv.at[0], to_chip(i)
            )
        slices[0, chip] = total[chip]

    def ascend_backward(make):
        for group in groups:
            for d in group:
                make(head_at(d))
            for d in group:
                add_up(1, mine + head_at(d), chips + head_at(d) * across)
            for offset in chip_offsets:
                if offset[0] in group:
                    i = chip_at(offset)
                    send_slice(
                        total.at[chips + i, sent_rows(1)], slices.at[1, chip, sent_rows(1)],
                        a_send.at[1], a_recv.at[1], to_chip(i),
                    )
        slices[1, chip] = total[chips + chip]

    def scan(turn):
        near_first, _, _, far_last = orders(turn)
        slices_whole(turn, chips - 1).wait_recv()
        running = jnp.zeros((rows, DH), F32)
        before = jnp.full((1, DH), -1.0, F32)
        for j in range(chips):
            i = j if turn == 0 else chips - 1 - j
            ids = slices[0, i, rows : rows + 8, :]
            enters = ids[near_first : near_first + 1, :]
            leaves = ids[far_last : far_last + 1, :]
            here = slice(i * rows, (i + 1) * rows)
            scanned[turn, here, :] = running * equal(before, enters)
            running = slices[turn, i, 0:rows, :] + running * equal(before, leaves)
            before = leaves
        for offset in chip_offsets:
            i = chip_at(offset)
            send_slice(
                scanned.at[turn, slot(i), :], landed.at[turn, slot(chip), :],
                b_send.at[turn], b_recv.at[turn, here_y], to_chip(i),
            )
        landed[turn, slot(chip), :] = scanned[turn, slot(chip), :]

    def descend(turn, into, then):
        near_first, near_last, far_first, _ = orders(turn)
        next_to = equal(ids_of(near_last), ids_of(far_first))
        through = equal(ids_of(near_first), ids_of(far_first))
        near = is_near(turn)
        own_enter = jnp.where(near, 1.0, through)
        own_sib = jnp.where(near, 0.0, next_to)
        sib_enter = jnp.where(near, through, 1.0)
        sib_own = jnp.where(near, next_to, 0.0)
        for group in reversed(groups):
            for d in group:
                head = head_at(d)
                at = cols(head)
                back_whole(turn, across - (d == 0), head).wait_recv()
                to_sib[turn, at, :] = (
                    landed[turn, at, :] * sib_enter + piece[turn, cols(mine + head), :] * sib_own
                )
                push_down(turn, head).start()
                beyond = sib_piece[turn, cols(mine + head), :]
                into(head, landed[turn, at, :] * own_enter + beyond * own_sib)
            for d in group:
                then(head_at(d))

    sib_ids = to_sibling(my_info, sib_info, sib_sem.at[0], sib_sem.at[1])

    def settle(turn):
        whole = to_sibling(
            to_sib.at[turn], from_sib.at[turn], down_send.at[turn], down_recv.at[turn, 0]
        )
        whole.wait_send()
        back_whole(turn, chips - 1, 0).wait_send()
        slices_whole(turn, chips - 1).wait_send()
        if turn == 0:
            up_half().wait_send()
            sib_ids.wait_send()
            for n in range(3):
                swap(n).wait_send()

    def make_piece(h):
        piece[0, cols(h), :] = tn(k[:, cols(h)] * last_col[...], v[:, cols(h)])

    ascend_forward()

    later = lax.broadcasted_iota(jnp.int32, (tokens, DH), 0)
    for b in range(blocks):
        block = slice(b * DH, (b + 1) * DH)
        earlier = lax.broadcasted_iota(jnp.int32, (tokens, DH), 1) + b * DH
        ids = jnp.broadcast_to(drow[:, block], (tokens, DH))
        same[:, block] = jnp.where((dcol[...] == ids) & (later >= earlier), 1.0, 0.0).astype(BF16)
    for copy in later_loads:
        copy.wait()

    def prepare(j, carry, base):
        h = base + j
        qf[:, cols(h)] = q[:, cols(h)] * first_col[...].astype(BF16)
        scaled[:, cols(h)] = gain[:, cols(h)] * dy[:, cols(h)].astype(F32)
        return carry

    def widen(j, carry):
        qf_wide[:, cols(j)] = qf[:, cols(other + j)].astype(F32)
        return carry

    lax.fori_loop(0, half, functools.partial(prepare, base=other), 0)
    lax.fori_loop(0, half, widen, 0)
    swap(0).start()
    swap(1).start()

    def local_forward(j, carry, base):
        h = base + j
        for r in range(tiles):
            here, upto = slice(r * TILE, (r + 1) * TILE), slice(0, (r + 1) * TILE)
            scores = nt(q[here, cols(h)], k[upto, cols(h)])
            masked = scores.astype(BF16) * same[here, upto]
            weights[h, here, upto] = masked
            att[here, cols(h)] = nn(masked, v[upto, cols(h)])
        return carry

    lax.fori_loop(0, half, functools.partial(local_forward, base=other), 0, unroll=2)
    swap(2).start()
    scan(0)
    lax.fori_loop(0, half, functools.partial(prepare, base=mine), 0)
    lax.fori_loop(0, half, functools.partial(local_forward, base=mine), 0, unroll=2)
    for n in range(3):
        swap(n).wait_recv()

    def turn_queries(j, carry):
        queries = qf_in[:, cols(j)].astype(BF16)
        qf_sib[:, cols(j)] = queries
        turned_sib[cols(j), :] = queries.T
        qf_turned[cols(j), :] = qf[:, cols(mine + j)].T
        return carry

    lax.fori_loop(0, half, turn_queries, 0)

    def enter(head, block):
        state[cols(mine + head), :] = block.astype(BF16)

    def attend(head):
        h = mine + head
        whole = att[:, cols(h)] + nn(qf[:, cols(h)], state[cols(h), :])
        att[:, cols(h)] = whole
        sq_acc[...] += whole * whole
        gr_acc[...] += scaled[:, cols(h)] * whole
        entering = to_sib[0, cols(head), :].astype(BF16)
        whole = att_sib[:, cols(head)] + nn(qf_sib[:, cols(head)], entering)
        att_sib[:, cols(head)] = whole
        sq_sib[...] += whole * whole
        gr_sib[...] += scaled_sib[:, cols(head)] * whole

    sq_acc[...] = jnp.zeros_like(sq_acc)
    gr_acc[...] = jnp.zeros_like(gr_acc)
    sq_sib[...] = jnp.zeros_like(sq_sib)
    gr_sib[...] = jnp.zeros_like(gr_sib)
    descend(0, enter, attend)
    for at, squares, grads in ((core, sq_acc, gr_acc), (1 - core, sq_sib, gr_sib)):
        square_sums, grad_sums = row_sums(squares[...]), row_sums(grads[...])
        for b in range(blocks):
            block = slice(b * DH, (b + 1) * DH)
            stat_out[at, b : b + 1, :] = square_sums[:, block]
            stat_out[at, blocks + b : blocks + b + 1, :] = grad_sums[:, block]

    def send_stat(device):
        pltpu.make_async_remote_copy(
            src_ref=stat_out,
            dst_ref=stat_in.at[2 * z + core],
            send_sem=stat_sem.at[0],
            recv_sem=stat_sem.at[1],
            device_id=device,
            device_id_type=MESH,
        ).start()

    for offset in head_offsets:
        for a in (core, 1 - core):
            send_stat({"ctx": 2 * chip + a, "head": lax.rem(z + offset, nhead)})
    send_stat({"ctx": sibling})
    stat_in[2 * z + core] = stat_out[...]
    settle(0)
    for d in reversed(row_offsets):
        head = head_at(d)
        push_down(0, head).wait_recv()
        state[cols(other + head), :] = from_sib[0, cols(head), :].astype(BF16)
    for j in range(half):
        att[:, cols(other + j)] += nn(qf[:, cols(other + j)], state[cols(other + j), :])
    stat_whole = to_sibling(
        stat_in.at[0 : 2 * nhead - 1], stat_in.at[0 : 2 * nhead - 1],
        stat_sem.at[0], stat_sem.at[1],
    )
    stat_whole.wait_recv()
    sums = stat_in[0]
    for at in range(1, 2 * nhead):
        sums = sums + stat_in[at]
    stat_sum[...] = sums / (width * nhead)
    for at, inv_to, adj_to in ((core, inv_col, adj_col), (1 - core, inv_sib, adj_sib)):
        means = stat_sum[at]
        inv = lax.rsqrt(means[0:blocks, :] + epsilon)
        factor = inv * inv * inv * means[blocks : 2 * blocks, :]
        turned = jnp.concatenate([inv, factor] * (DH // (2 * blocks)), axis=0).T
        for b in range(blocks):
            block = slice(b * DH, (b + 1) * DH)
            inv_to[block, :] = jnp.broadcast_to(turned[:, b : b + 1], (DH, DH))
            adj_to[block, :] = jnp.broadcast_to(
                turned[:, blocks + b : blocks + b + 1], (DH, DH)
            )

    def adjoint(h):
        return (inv_col[...] * scaled[:, cols(h)] - att[:, cols(h)] * adj_col[...]).astype(BF16)

    def back_pieces(head):
        grads = adjoint(mine + head)
        oa[:, cols(mine + head)] = grads
        piece[1, cols(mine + head), :] = nn(qf_turned[cols(head), :], grads)
        grads = (
            inv_sib[...] * scaled_sib[:, cols(head)] - att_sib[:, cols(head)] * adj_sib[...]
        ).astype(BF16)
        sib_piece[1, cols(mine + head), :] = nn(turned_sib[cols(head), :], grads)

    ascend_backward(back_pieces)
    for j in range(half):
        oa[:, cols(other + j)] = adjoint(other + j)

    def local_backward(j, carry, base, kgl, vgl):
        h = base + j
        kl[:, cols(h)] = k[:, cols(h)] * last_col[...]
        vl[:, cols(h)] = v[:, cols(h)] * last_col[...]
        grads = oa[:, cols(h)]
        stepped = nt(grads, state[cols(h), :]) * first_col[...]
        for r in range(tiles):
            here, upto = slice(r * TILE, (r + 1) * TILE), slice(0, (r + 1) * TILE)
            scores = nt(grads[here], v[upto, cols(h)])
            masked = scores.astype(BF16) * same[here, upto]
            adj[here, upto] = masked
            qg[here, cols(h)] = (nn(masked, k[upto, cols(h)]) + stepped[here]).astype(BF16)
        for r in range(tiles):
            here, onward = slice(r * TILE, (r + 1) * TILE), slice(r * TILE, tokens)
            kgl[here, cols(j)] = tn(adj[onward, here], q[onward, cols(h)])
            vgl[here, cols(j)] = tn(weights[h, onward, here], grads[onward])
        normed[:, cols(h)] = (gain[:, cols(h)] * att[:, cols(h)] * inv_col[...]).astype(BF16)
        return carry

    lower = functools.partial(local_backward, base=0, kgl=kgl0, vgl=vgl0)
    upper = functools.partial(local_backward, base=half, kgl=kgl1, vgl=vgl1)
    lax.fori_loop(0, half, lower, 0, unroll=2)
    scan(1)
    lax.fori_loop(0, half, upper, 0, unroll=2)

    def enter_back(head, block):
        back_state[cols(mine + head), :] = block.astype(BF16)

    descend(1, enter_back, lambda head: None)
    stat_whole.wait_send()
    for d in reversed(row_offsets):
        head = head_at(d)
        push_down(1, head).wait_recv()
        back_state[cols(other + head), :] = from_sib[1, cols(head), :].astype(BF16)
    settle(1)


def finish(
    normed, qg, kgl0, kgl1, vgl0, vgl1, kl, vl, back_state,
    normed_hbm, qg_hbm, kg_hbm, vg_hbm,
    kg, vg, out_sem,
):
    heads = kg.shape[1] // DH
    stores = [
        pltpu.make_async_copy(normed, normed_hbm, out_sem.at[0]),
        pltpu.make_async_copy(qg, qg_hbm, out_sem.at[1]),
    ]
    for copy in stores:
        copy.start()
    parts = 2
    per_part = heads // parts
    for part, (kgl, vgl) in enumerate(((kgl0, vgl0), (kgl1, vgl1))):
        for j in range(per_part):
            here = slice(j * DH, (j + 1) * DH)
            at = slice((part * per_part + j) * DH, (part * per_part + j + 1) * DH)
            back = back_state[at, :]
            kg[:, at] = (kgl[:, here] + nt(vl[:, at], back)).astype(BF16)
            vg[:, at] = (vgl[:, here] + nn(kl[:, at], back)).astype(BF16)
        done = slice(part * per_part * DH, (part + 1) * per_part * DH)
        for i, (src, dst) in enumerate(((kg, kg_hbm), (vg, vg_hbm))):
            copy = pltpu.make_async_copy(
                src.at[:, done], dst.at[:, done], out_sem.at[2 + 2 * part + i]
            )
            copy.start()
            stores.append(copy)
    for copy in stores:
        copy.wait()


def body(nctx, nhead, query_rows, key_rows, value_rows, out_grad, norm_gain, doc_ids):
    tokens, width = query_rows.shape
    heads = width // DH
    half = heads // 2
    chips = nctx // 2
    rows = half * DH // chips
    blocks = tokens // DH
    grid = (tokens, width)
    half_grid = (tokens, width // 2)
    dma = pltpu.SemaphoreType.DMA
    scratch = [
        *[pltpu.VMEM(grid, BF16)] * 6,
        *[pltpu.VMEM(grid, F32)] * 2,
        pltpu.VMEM((heads, tokens, tokens), BF16),
        pltpu.VMEM((tokens, tokens), BF16),
        pltpu.VMEM((tokens, tokens), BF16),
        pltpu.VMEM((1, width), F32),
        pltpu.VMEM((1, tokens), jnp.int32),
        pltpu.VMEM((half * DH, tokens), BF16),
        *[pltpu.VMEM((tokens, DH), F32)] * 2,
        pltpu.VMEM((tokens, DH), BF16),
        *[pltpu.VMEM((tokens, DH), F32)] * 4,
        pltpu.VMEM((2, heads * DH, DH), F32),
        pltpu.VMEM((2, heads * DH, DH), F32),
        pltpu.VMEM((2 * chips, rows + 8, DH), F32),
        pltpu.VMEM((2, chips, rows + 8, DH), F32),
        *[pltpu.VMEM((2, half * DH, DH), F32)] * 4,
        pltpu.VMEM((heads * DH, DH), BF16),
        *[pltpu.VMEM((8, DH), F32)] * 3,
        pltpu.VMEM((2, 2 * blocks, DH), F32),
        pltpu.VMEM((2 * nhead, 2, 2 * blocks, DH), F32),
        pltpu.VMEM((2, 2 * blocks, DH), F32),
        *[pltpu.VMEM(half_grid, F32)] * 4,
        pltpu.VMEM(half_grid, BF16),
        pltpu.VMEM((half * DH, tokens), BF16),
        *[pltpu.VMEM((tokens, DH), F32)] * 4,
        dma((8,)),
        *[dma((2,))] * 2,
        pltpu.SemaphoreType.REGULAR,
        *[dma((2,))] * 3,
        dma((2, half)),
        dma((2,)),
        dma((2, half)),
        dma((2,)),
        *[dma((3,))] * 2,
    ]
    arrays = (
        query_rows, key_rows, value_rows, out_grad,
        norm_gain.reshape(1, width), doc_ids.reshape(1, tokens),
    )
    anywhere = pl.BlockSpec(memory_space=pl.ANY)
    in_hbm = pl.BlockSpec(memory_space=pltpu.HBM)
    in_vmem = pl.BlockSpec(memory_space=pltpu.VMEM)
    parts = pl.pallas_call(
        functools.partial(kernel, nctx, nhead),
        out_shape=[
            *[jax.ShapeDtypeStruct(grid, BF16)] * 2,
            *[jax.ShapeDtypeStruct(half_grid, F32)] * 4,
            *[jax.ShapeDtypeStruct(grid, BF16)] * 2,
            jax.ShapeDtypeStruct((heads * DH, DH), BF16),
        ],
        in_specs=[in_hbm] * 6,
        out_specs=[in_vmem] * 9,
        scratch_shapes=scratch,
        compiler_params=pltpu.CompilerParams(
            collective_id=0, has_side_effects=True, vmem_limit_bytes=44 * 2**20
        ),
        name="attend",
    )(*[pltpu.with_memory_space_constraint(array, pltpu.HBM) for array in arrays])
    return pl.pallas_call(
        finish,
        out_shape=[jax.ShapeDtypeStruct(grid, BF16)] * 4,
        in_specs=[in_vmem] * 9,
        out_specs=[anywhere] * 4,
        scratch_shapes=[*[pltpu.VMEM(grid, BF16)] * 2, dma((6,))],
        compiler_params=pltpu.CompilerParams(vmem_limit_bytes=16 * 2**20),
        name="finish",
    )(*parts)


def solution(mesh):
    nctx, nhead = mesh.shape["ctx"], mesh.shape["head"]
    placed = (
        P("ctx", "head"),
        P("ctx", "head"),
        P("ctx", "head"),
        P("ctx", "head"),
        P("head"),
        P("ctx"),
    )
    return jax.shard_map(
        functools.partial(body, nctx, nhead),
        mesh=mesh,
        in_specs=placed,
        out_specs=(P("ctx", "head"), P("ctx", "head"), P("ctx", "head"), P("ctx", "head")),
        check_vma=False,
    )
```

```python
import functools
import math

import jax
import jax.numpy as jnp
from jax import lax
from jax.experimental import pallas as pl
from jax.experimental.pallas import tpu as pltpu
from jax.sharding import PartitionSpec as P

DH = 128
TILE = 256
epsilon = 1e-05
MESH = pl.DeviceIdType.MESH
F32 = jnp.float32
BF16 = jnp.bfloat16


def nn(a, b):
    return lax.dot_general(a, b, (((1,), (0,)), ((), ())), preferred_element_type=F32)


def nt(a, b):
    return lax.dot_general(a, b, (((1,), (1,)), ((), ())), preferred_element_type=F32)


def tn(a, b):
    return lax.dot_general(a, b, (((0,), (0,)), ((), ())), preferred_element_type=F32)


def equal(a, b):
    return jnp.where(a == b, 1.0, 0.0).astype(F32)


def row_sums(values):
    ones = jnp.ones((8, DH), BF16)
    high = values.astype(BF16)
    low = (values - high.astype(F32)).astype(BF16)
    return (nt(ones, high) + nt(ones, low))[0:1, :]


def far_first(chips):
    across = math.isqrt(chips)
    along = chips // across

    def hops(offset):
        dy, dx = offset
        return min(dy, along - dy) + min(dx, across - dx)

    offsets = [(dy, dx) for dy in range(along) for dx in range(across) if dy + dx > 0]
    ordered = []
    for dy, dx in sorted(offsets, key=hops, reverse=True):
        for offset in ((dy, dx), (-dy % along, -dx % across)):
            if offset not in ordered:
                ordered.append(offset)
    return ordered


def kernel(
    nctx, nhead,
    q_hbm, k_hbm, v_hbm, dy_hbm, gain_hbm, docs_hbm,
    normed, qg, kgl0, kgl1, vgl0, vgl1, kl, vl, back_state,
    q, k, v, dy, qf, oa, att, scaled, weights, adj, same, gain, docs, qf_turned, dcol,
    first_col, last_col, inv_col, adj_col, sq_acc, gr_acc,
    piece, sib_piece, total, slices, scanned, landed, to_sib, from_sib, state,
    my_info, sib_info, chip_info, stat_out, stat_in, stat_sum,
    qf_wide, qf_in, att_sib, scaled_sib, qf_sib, turned_sib,
    sq_sib, gr_sib, inv_sib, adj_sib,
    in_sem, sib_sem, up_sem, go_sem, a_send, a_recv, b_send, b_recv,
    down_send, down_recv, stat_sem, swap_send, swap_recv,
):
    tokens, width = q.shape
    heads = width // DH
    half = heads // 2
    chips = nctx // 2
    across = math.isqrt(chips)
    along = chips // across
    rows = half * DH // chips
    blocks = tokens // DH
    tiles = tokens // TILE
    me = lax.axis_index("ctx")
    z = lax.axis_index("head")
    chip = lax.div(me, 2)
    core = lax.rem(me, 2)
    sibling = me + 1 - 2 * core
    mine, other = core * half, (1 - core) * half
    here_y, here_x = lax.div(chip, across), lax.rem(chip, across)
    row_offsets = sorted(range(along), key=lambda d: -min(d, along - d))
    groups = [row_offsets[:1], row_offsets[1:-1], row_offsets[-1:]]
    column_offsets = sorted(range(across), key=lambda d: -min(d, across - d))

    def cols(h):
        return pl.ds(pl.multiple_of(h * DH, DH), DH)

    def side(s):
        return pl.ds(pl.multiple_of(s * (width // 2), width // 2), width // 2)

    def slot(i):
        return pl.ds(pl.multiple_of(i * rows, rows), rows)

    def chip_at(offset):
        y = lax.rem(here_y + offset[0], along)
        x = lax.rem(here_x + offset[1], across)
        return y * across + x

    def head_at(d):
        return lax.rem(here_y + d, along)

    def to_chip(i):
        return {"ctx": 2 * i + core}

    chip_offsets = far_first(chips)
    head_offsets = sorted(range(1, nhead), key=lambda d: -min(d, nhead - d))

    def load(i, src, dst, s):
        return pltpu.make_async_copy(src.at[:, side(s)], dst.at[:, side(s)], in_sem.at[i])

    first_loads = [load(0, k_hbm, k, 1 - core), load(1, v_hbm, v, 1 - core)]
    docs_load = pltpu.make_async_copy(docs_hbm, docs, in_sem.at[2])
    own_loads = [load(3, k_hbm, k, core), load(4, v_hbm, v, core)]
    later_loads = [
        pltpu.make_async_copy(q_hbm, q, in_sem.at[5]),
        pltpu.make_async_copy(dy_hbm, dy, in_sem.at[6]),
        pltpu.make_async_copy(gain_hbm, gain, in_sem.at[7]),
    ]
    docs_load.start()
    for copy in first_loads + own_loads:
        copy.start()

    barrier = pltpu.get_barrier_semaphore()

    def greet(device):
        pl.semaphore_signal(barrier, inc=1, device_id=device, device_id_type=MESH)

    for offset in chip_offsets:
        greet({"ctx": 2 * chip_at(offset)})
    for offset in head_offsets:
        greet({"ctx": 2 * chip, "head": lax.rem(z + offset, nhead)})
    greet({"ctx": sibling})
    for copy in later_loads:
        copy.start()

    docs_load.wait()
    drow = docs[...].astype(F32)
    first_id = drow[:, 0:1]
    last_id = drow[:, tokens - 1 : tokens]
    my_info[0:1, :] = jnp.broadcast_to(first_id, (1, DH))
    my_info[1:2, :] = jnp.broadcast_to(last_id, (1, DH))
    for b in range(blocks):
        block = slice(b * DH, (b + 1) * DH)
        dcol[block, :] = jnp.broadcast_to(drow[:, block], (DH, DH)).T
    first_col[...] = equal(dcol[...], first_id)
    last_col[...] = equal(dcol[...], last_id).astype(BF16)

    def to_sibling(src, dst, send_sem, recv_sem):
        return pltpu.make_async_remote_copy(
            src_ref=src,
            dst_ref=dst,
            send_sem=send_sem,
            recv_sem=recv_sem,
            device_id={"ctx": sibling},
            device_id_type=MESH,
        )

    def up_half():
        at = pl.ds(pl.multiple_of(other * DH, half * DH), half * DH)
        return to_sibling(piece.at[0, at, :], sib_piece.at[0, at, :], up_sem.at[0], up_sem.at[1])

    def push_down(turn, head):
        return to_sibling(
            to_sib.at[turn, cols(head), :], from_sib.at[turn, cols(head), :],
            down_send.at[turn], down_recv.at[turn, head],
        )

    def send_slice(src, dst, send_sem, recv_sem, device):
        pltpu.make_async_remote_copy(
            src_ref=src,
            dst_ref=dst,
            send_sem=send_sem,
            recv_sem=recv_sem,
            device_id=device,
            device_id_type=MESH,
        ).start()

    def sent_rows(turn):
        return slice(0, rows + 8) if turn == 0 else slice(0, rows)

    def slices_whole(turn, count):
        part = (slice(0, count), sent_rows(turn))
        return to_sibling(total.at[part], total.at[part], a_send.at[turn], a_recv.at[turn])

    def back_whole(turn, count, row):
        part = (turn, slice(0, count * rows))
        return to_sibling(
            scanned.at[part], landed.at[part], b_send.at[turn], b_recv.at[turn, row]
        )

    def swap(n):
        src, dst = (
            (scaled.at[:, side(1 - core)], scaled_sib),
            (qf_wide, qf_in),
            (att.at[:, side(1 - core)], att_sib),
        )[n]
        return to_sibling(src, dst, swap_send.at[n], swap_recv.at[n])

    def orders(turn):
        return (0, 1, 2, 3) if turn == 0 else (3, 2, 1, 0)

    def is_near(turn):
        return jnp.full((1, DH), core if turn == 0 else 1 - core, jnp.int32) == 0

    def ids_of(row):
        return chip_info[row : row + 1, :]

    def add_up(turn, head, place):
        _, near_last, _, far_last = orders(turn)
        joined = equal(ids_of(near_last), ids_of(far_last))
        own_share = jnp.where(is_near(turn), joined, 1.0)
        sib_share = jnp.where(is_near(turn), 1.0, joined)
        for x in range(across):
            part = pl.ds(pl.multiple_of(head * DH + x * rows, rows), rows)
            total[place + x, 0:rows, :] = (
                piece[turn, part, :] * own_share + sib_piece[turn, part, :] * sib_share
            )

    def ascend_forward():
        for copy in first_loads:
            copy.wait()
        for j in range(half):
            make_piece(other + j)

        @pl.when(core == 1)
        def _():
            pl.semaphore_wait(barrier, 1)
            sib_ids.start()
            up_half().start()

        for copy in own_loads:
            copy.wait()

        @pl.when(core == 0)
        def _():
            sib_ids.wait_recv()
            sib_ids.start()
            up_half().start()

        for j in range(half):
            make_piece(mine + j)

        @pl.when(core == 1)
        def _():
            sib_ids.wait_recv()

        near = is_near(0)
        for at in range(2):
            here, there = my_info[at : at + 1, :], sib_info[at : at + 1, :]
            chip_info[at : at + 1, :] = jnp.where(near, here, there)
            chip_info[at + 2 : at + 3, :] = jnp.where(near, there, here)
        for i in range(chips):
            total[i, rows : rows + 8, :] = chip_info[...]
        up_half().wait_recv()
        for head in range(half):
            add_up(0, mine + head, head * across)

        @pl.when(core == 0)
        def _():
            pl.semaphore_wait(barrier, 1 + 2 * (chips - 1) + 2 * (nhead - 1))
            pl.semaphore_signal(go_sem, inc=1, device_id={"ctx": sibling}, device_id_type=MESH)

        @pl.when(core == 1)
        def _():
            pl.semaphore_wait(go_sem, 1)

        for offset in chip_offsets:
            i = chip_at(offset)
            send_slice(
                total.at[i], slices.at[0, chip], a_send.at[0], a_recv.at[0], to_chip(i)
            )
        slices[0, chip] = total[chip]

    def ascend_backward(make):
        for group in groups:
            for d in group:
                make(head_at(d))
            for d in group:
                add_up(1, mine + head_at(d), chips + head_at(d) * across)
            for offset in chip_offsets:
                if offset[0] in group:
                    i = chip_at(offset)
                    send_slice(
                        total.at[chips + i, sent_rows(1)], slices.at[1, chip, sent_rows(1)],
                        a_send.at[1], a_recv.at[1], to_chip(i),
                    )
        slices[1, chip] = total[chips + chip]

    def scan(turn):
        near_first, _, _, far_last = orders(turn)
        slices_whole(turn, chips - 1).wait_recv()
        running = jnp.zeros((rows, DH), F32)
        before = jnp.full((1, DH), -1.0, F32)
        for j in range(chips):
            i = j if turn == 0 else chips - 1 - j
            ids = slices[0, i, rows : rows + 8, :]
            enters = ids[near_first : near_first + 1, :]
            leaves = ids[far_last : far_last + 1, :]
            here = slice(i * rows, (i + 1) * rows)
            scanned[turn, here, :] = running * equal(before, enters)
            running = slices[turn, i, 0:rows, :] + running * equal(before, leaves)
            before = leaves
        for offset in chip_offsets:
            i = chip_at(offset)
            send_slice(
                scanned.at[turn, slot(i), :], landed.at[turn, slot(chip), :],
                b_send.at[turn], b_recv.at[turn, here_y], to_chip(i),
            )
        landed[turn, slot(chip), :] = scanned[turn, slot(chip), :]

    def descend(turn, into, then):
        near_first, near_last, far_first, _ = orders(turn)
        next_to = equal(ids_of(near_last), ids_of(far_first))
        through = equal(ids_of(near_first), ids_of(far_first))
        near = is_near(turn)
        own_enter = jnp.where(near, 1.0, through)
        own_sib = jnp.where(near, 0.0, next_to)
        sib_enter = jnp.where(near, through, 1.0)
        sib_own = jnp.where(near, next_to, 0.0)
        for group in reversed(groups):
            for d in group:
                head = head_at(d)
                at = cols(head)
                back_whole(turn, across - (d == 0), head).wait_recv()
                to_sib[turn, at, :] = (
                    landed[turn, at, :] * sib_enter + piece[turn, cols(mine + head), :] * sib_own
                )
                push_down(turn, head).start()
                beyond = sib_piece[turn, cols(mine + head), :]
                into(head, landed[turn, at, :] * own_enter + beyond * own_sib)
            for d in group:
                then(head_at(d))

    sib_ids = to_sibling(my_info, sib_info, sib_sem.at[0], sib_sem.at[1])

    def settle(turn):
        whole = to_sibling(
            to_sib.at[turn], from_sib.at[turn], down_send.at[turn], down_recv.at[turn, 0]
        )
        whole.wait_send()
        back_whole(turn, chips - 1, 0).wait_send()
        slices_whole(turn, chips - 1).wait_send()
        if turn == 0:
            up_half().wait_send()
            sib_ids.wait_send()
            for n in range(3):
                swap(n).wait_send()

    def make_piece(h):
        piece[0, cols(h), :] = tn(k[:, cols(h)] * last_col[...], v[:, cols(h)])

    ascend_forward()

    later = lax.broadcasted_iota(jnp.int32, (tokens, DH), 0)
    for b in range(blocks):
        block = slice(b * DH, (b + 1) * DH)
        earlier = lax.broadcasted_iota(jnp.int32, (tokens, DH), 1) + b * DH
        ids = jnp.broadcast_to(drow[:, block], (tokens, DH))
        same[:, block] = jnp.where((dcol[...] == ids) & (later >= earlier), 1.0, 0.0).astype(BF16)
    for copy in later_loads:
        copy.wait()

    def prepare(j, carry, base):
        h = base + j
        qf[:, cols(h)] = q[:, cols(h)] * first_col[...].astype(BF16)
        scaled[:, cols(h)] = gain[:, cols(h)] * dy[:, cols(h)].astype(F32)
        return carry

    def widen(j, carry):
        qf_wide[:, cols(j)] = qf[:, cols(other + j)].astype(F32)
        return carry

    lax.fori_loop(0, half, functools.partial(prepare, base=other), 0)
    lax.fori_loop(0, half, widen, 0)
    swap(0).start()
    swap(1).start()

    def local_forward(j, carry, base):
        h = base + j
        for r in range(tiles):
            here, upto = slice(r * TILE, (r + 1) * TILE), slice(0, (r + 1) * TILE)
            scores = nt(q[here, cols(h)], k[upto, cols(h)])
            masked = scores.astype(BF16) * same[here, upto]
            weights[h, here, upto] = masked
            att[here, cols(h)] = nn(masked, v[upto, cols(h)])
        return carry

    lax.fori_loop(0, half, functools.partial(local_forward, base=other), 0, unroll=2)
    swap(2).start()
    scan(0)
    lax.fori_loop(0, half, functools.partial(prepare, base=mine), 0)
    lax.fori_loop(0, half, functools.partial(local_forward, base=mine), 0, unroll=2)
    for n in range(3):
        swap(n).wait_recv()

    def turn_queries(j, carry):
        queries = qf_in[:, cols(j)].astype(BF16)
        qf_sib[:, cols(j)] = queries
        turned_sib[cols(j), :] = queries.T
        qf_turned[cols(j), :] = qf[:, cols(mine + j)].T
        return carry

    lax.fori_loop(0, half, turn_queries, 0)

    def enter(head, block):
        state[cols(mine + head), :] = block.astype(BF16)

    def attend(head):
        h = mine + head
        whole = att[:, cols(h)] + nn(qf[:, cols(h)], state[cols(h), :])
        att[:, cols(h)] = whole
        sq_acc[...] += whole * whole
        gr_acc[...] += scaled[:, cols(h)] * whole
        entering = to_sib[0, cols(head), :].astype(BF16)
        whole = att_sib[:, cols(head)] + nn(qf_sib[:, cols(head)], entering)
        att_sib[:, cols(head)] = whole
        sq_sib[...] += whole * whole
        gr_sib[...] += scaled_sib[:, cols(head)] * whole

    sq_acc[...] = jnp.zeros_like(sq_acc)
    gr_acc[...] = jnp.zeros_like(gr_acc)
    sq_sib[...] = jnp.zeros_like(sq_sib)
    gr_sib[...] = jnp.zeros_like(gr_sib)
    descend(0, enter, attend)
    for at, squares, grads in ((core, sq_acc, gr_acc), (1 - core, sq_sib, gr_sib)):
        square_sums, grad_sums = row_sums(squares[...]), row_sums(grads[...])
        for b in range(blocks):
            block = slice(b * DH, (b + 1) * DH)
            stat_out[at, b : b + 1, :] = square_sums[:, block]
            stat_out[at, blocks + b : blocks + b + 1, :] = grad_sums[:, block]

    def send_stat(device):
        pltpu.make_async_remote_copy(
            src_ref=stat_out,
            dst_ref=stat_in.at[2 * z + core],
            send_sem=stat_sem.at[0],
            recv_sem=stat_sem.at[1],
            device_id=device,
            device_id_type=MESH,
        ).start()

    for offset in head_offsets:
        for a in (core, 1 - core):
            send_stat({"ctx": 2 * chip + a, "head": lax.rem(z + offset, nhead)})
    send_stat({"ctx": sibling})
    stat_in[2 * z + core] = stat_out[...]
    settle(0)
    for d in reversed(row_offsets):
        head = head_at(d)
        push_down(0, head).wait_recv()
        state[cols(other + head), :] = from_sib[0, cols(head), :].astype(BF16)
    for j in range(half):
        att[:, cols(other + j)] += nn(qf[:, cols(other + j)], state[cols(other + j), :])
    stat_whole = to_sibling(
        stat_in.at[0 : 2 * nhead - 1], stat_in.at[0 : 2 * nhead - 1],
        stat_sem.at[0], stat_sem.at[1],
    )
    stat_whole.wait_recv()
    sums = stat_in[0]
    for at in range(1, 2 * nhead):
        sums = sums + stat_in[at]
    stat_sum[...] = sums / (width * nhead)
    for at, inv_to, adj_to in ((core, inv_col, adj_col), (1 - core, inv_sib, adj_sib)):
        means = stat_sum[at]
        inv = lax.rsqrt(means[0:blocks, :] + epsilon)
        factor = inv * inv * inv * means[blocks : 2 * blocks, :]
        turned = jnp.concatenate([inv, factor] * (DH // (2 * blocks)), axis=0).T
        for b in range(blocks):
            block = slice(b * DH, (b + 1) * DH)
            inv_to[block, :] = jnp.broadcast_to(turned[:, b : b + 1], (DH, DH))
            adj_to[block, :] = jnp.broadcast_to(
                turned[:, blocks + b : blocks + b + 1], (DH, DH)
            )

    def adjoint(h):
        return (inv_col[...] * scaled[:, cols(h)] - att[:, cols(h)] * adj_col[...]).astype(BF16)

    def back_pieces(head):
        grads = adjoint(mine + head)
        oa[:, cols(mine + head)] = grads
        piece[1, cols(mine + head), :] = nn(qf_turned[cols(head), :], grads)
        grads = (
            inv_sib[...] * scaled_sib[:, cols(head)] - att_sib[:, cols(head)] * adj_sib[...]
        ).astype(BF16)
        sib_piece[1, cols(mine + head), :] = nn(turned_sib[cols(head), :], grads)

    ascend_backward(back_pieces)
    for j in range(half):
        oa[:, cols(other + j)] = adjoint(other + j)

    def local_backward(j, carry, base, kgl, vgl):
        h = base + j
        kl[:, cols(h)] = k[:, cols(h)] * last_col[...]
        vl[:, cols(h)] = v[:, cols(h)] * last_col[...]
        grads = oa[:, cols(h)]
        stepped = nt(grads, state[cols(h), :]) * first_col[...]
        for r in range(tiles):
            here, upto = slice(r * TILE, (r + 1) * TILE), slice(0, (r + 1) * TILE)
            scores = nt(grads[here], v[upto, cols(h)])
            masked = scores.astype(BF16) * same[here, upto]
            adj[here, upto] = masked
            qg[here, cols(h)] = (nn(masked, k[upto, cols(h)]) + stepped[here]).astype(BF16)
        for r in range(tiles):
            here, onward = slice(r * TILE, (r + 1) * TILE), slice(r * TILE, tokens)
            kgl[here, cols(j)] = tn(adj[onward, here], q[onward, cols(h)])
            vgl[here, cols(j)] = tn(weights[h, onward, here], grads[onward])
        normed[:, cols(h)] = (gain[:, cols(h)] * att[:, cols(h)] * inv_col[...]).astype(BF16)
        return carry

    lower = functools.partial(local_backward, base=0, kgl=kgl0, vgl=vgl0)
    upper = functools.partial(local_backward, base=half, kgl=kgl1, vgl=vgl1)
    lax.fori_loop(0, half, lower, 0, unroll=2)
    scan(1)
    lax.fori_loop(0, half, upper, 0, unroll=2)

    def enter_back(head, block):
        back_state[cols(mine + head), :] = block.astype(BF16)

    descend(1, enter_back, lambda head: None)
    stat_whole.wait_send()
    for d in reversed(row_offsets):
        head = head_at(d)
        push_down(1, head).wait_recv()
        back_state[cols(other + head), :] = from_sib[1, cols(head), :].astype(BF16)
    settle(1)


def finish(
    normed, qg, kgl0, kgl1, vgl0, vgl1, kl, vl, back_state,
    normed_hbm, qg_hbm, kg_hbm, vg_hbm,
    kg, vg, out_sem,
):
    heads = kg.shape[1] // DH
    stores = [
        pltpu.make_async_copy(normed, normed_hbm, out_sem.at[0]),
        pltpu.make_async_copy(qg, qg_hbm, out_sem.at[1]),
    ]
    for copy in stores:
        copy.start()
    part = 2
    for first in range(0, heads, part):
        kgl, vgl = (kgl0, vgl0) if first < heads // 2 else (kgl1, vgl1)
        for h in range(first, first + part):
            j = h % (heads // 2)
            here, at = slice(j * DH, (j + 1) * DH), slice(h * DH, (h + 1) * DH)
            back = back_state[at, :]
            kg[:, at] = (kgl[:, here] + nt(vl[:, at], back)).astype(BF16)
            vg[:, at] = (vgl[:, here] + nn(kl[:, at], back)).astype(BF16)
        done = slice(first * DH, (first + part) * DH)
        for i, (src, dst) in enumerate(((kg, kg_hbm), (vg, vg_hbm))):
            copy = pltpu.make_async_copy(src.at[:, done], dst.at[:, done], out_sem.at[2 + first + i])
            copy.start()
            stores.append(copy)
    for copy in stores:
        copy.wait()


def body(nctx, nhead, query_rows, key_rows, value_rows, out_grad, norm_gain, doc_ids):
    tokens, width = query_rows.shape
    heads = width // DH
    half = heads // 2
    chips = nctx // 2
    rows = half * DH // chips
    blocks = tokens // DH
    grid = (tokens, width)
    half_grid = (tokens, width // 2)
    dma = pltpu.SemaphoreType.DMA
    scratch = [
        *[pltpu.VMEM(grid, BF16)] * 6,
        *[pltpu.VMEM(grid, F32)] * 2,
        pltpu.VMEM((heads, tokens, tokens), BF16),
        pltpu.VMEM((tokens, tokens), BF16),
        pltpu.VMEM((tokens, tokens), BF16),
        pltpu.VMEM((1, width), F32),
        pltpu.VMEM((1, tokens), jnp.int32),
        pltpu.VMEM((half * DH, tokens), BF16),
        *[pltpu.VMEM((tokens, DH), F32)] * 2,
        pltpu.VMEM((tokens, DH), BF16),
        *[pltpu.VMEM((tokens, DH), F32)] * 4,
        pltpu.VMEM((2, heads * DH, DH), F32),
        pltpu.VMEM((2, heads * DH, DH), F32),
        pltpu.VMEM((2 * chips, rows + 8, DH), F32),
        pltpu.VMEM((2, chips, rows + 8, DH), F32),
        *[pltpu.VMEM((2, half * DH, DH), F32)] * 4,
        pltpu.VMEM((heads * DH, DH), BF16),
        *[pltpu.VMEM((8, DH), F32)] * 3,
        pltpu.VMEM((2, 2 * blocks, DH), F32),
        pltpu.VMEM((2 * nhead, 2, 2 * blocks, DH), F32),
        pltpu.VMEM((2, 2 * blocks, DH), F32),
        *[pltpu.VMEM(half_grid, F32)] * 4,
        pltpu.VMEM(half_grid, BF16),
        pltpu.VMEM((half * DH, tokens), BF16),
        *[pltpu.VMEM((tokens, DH), F32)] * 4,
        dma((8,)),
        *[dma((2,))] * 2,
        pltpu.SemaphoreType.REGULAR,
        *[dma((2,))] * 3,
        dma((2, half)),
        dma((2,)),
        dma((2, half)),
        dma((2,)),
        *[dma((3,))] * 2,
    ]
    arrays = (
        query_rows, key_rows, value_rows, out_grad,
        norm_gain.reshape(1, width), doc_ids.reshape(1, tokens),
    )
    anywhere = pl.BlockSpec(memory_space=pl.ANY)
    in_hbm = pl.BlockSpec(memory_space=pltpu.HBM)
    in_vmem = pl.BlockSpec(memory_space=pltpu.VMEM)
    parts = pl.pallas_call(
        functools.partial(kernel, nctx, nhead),
        out_shape=[
            *[jax.ShapeDtypeStruct(grid, BF16)] * 2,
            *[jax.ShapeDtypeStruct(half_grid, F32)] * 4,
            *[jax.ShapeDtypeStruct(grid, BF16)] * 2,
            jax.ShapeDtypeStruct((heads * DH, DH), BF16),
        ],
        in_specs=[in_hbm] * 6,
        out_specs=[in_vmem] * 9,
        scratch_shapes=scratch,
        compiler_params=pltpu.CompilerParams(
            collective_id=0, has_side_effects=True, vmem_limit_bytes=44 * 2**20
        ),
        name="attend",
    )(*[pltpu.with_memory_space_constraint(array, pltpu.HBM) for array in arrays])
    return pl.pallas_call(
        finish,
        out_shape=[jax.ShapeDtypeStruct(grid, BF16)] * 4,
        in_specs=[in_vmem] * 9,
        out_specs=[anywhere] * 4,
        scratch_shapes=[*[pltpu.VMEM(grid, BF16)] * 2, dma((2 + heads,))],
        compiler_params=pltpu.CompilerParams(vmem_limit_bytes=16 * 2**20),
        name="finish",
    )(*parts)


def solution(mesh):
    nctx, nhead = mesh.shape["ctx"], mesh.shape["head"]
    placed = (
        P("ctx", "head"),
        P("ctx", "head"),
        P("ctx", "head"),
        P("ctx", "head"),
        P("head"),
        P("ctx"),
    )
    return jax.shard_map(
        functools.partial(body, nctx, nhead),
        mesh=mesh,
        in_specs=placed,
        out_specs=(P("ctx", "head"), P("ctx", "head"), P("ctx", "head"), P("ctx", "head")),
        check_vma=False,
    )
```
